32 devices in a mesh: gene: 4 (over y, x), sample: 2 (over core), variant: 4 (over z).
Axes of the slice: x: 2, y: 2, z: 4, core: 2. Of those that a mesh axis runs over, the one named last changes fastest.
Arguments:
- expression: bfloat16 [8192, 4096], P('sample', 'gene'), may hold values from -6 to 6
- profile: float32 [4096, 7], P('gene'), may hold values from -0.25 to 0.25
- dosage: int32 [8192, 512], P('sample', 'variant'), may hold values from 0 to 2
- signature: int32 [500], replicated, may hold values from 0 to 4095, as said below
Outputs:
- interaction: float32 [3584, 4096], P(('variant', 'sample'), 'gene')
- proportions: float32 [8192, 7], P('sample')
The draws below stay inside these ranges and needn't reach their ends.
Inputs may be any that keep to these rules, and one draw needn't show every extreme that they name: `signature`: distinct gene indices; gene 0 and gene 4096 - 1 are always among them.
All inputs are finite; a program needn't handle non-finite values.
Results may differ from the reference program's by a relative error of at most 0.0045.
Values sent between devices are 32-bit elements; how exact they have to be, the bound alone decides.
No kernel may reach another device: no remote copies, remote signals or barrier semaphores. Data moves between devices by JAX's collectives and lax.ppermute only.
A program may use at most 128 MiB of HBM per device.

```python
import math
import jax
import jax.numpy as jnp
from jax import lax

GENES = 4096
SIG = 500
K = 7
V_DEV = 128
SAMPLES = 8192
VARIANTS = 512
N_VARIANT = 4


def draw_signature(key, part):
    first = jax.random.permutation(jax.random.fold_in(key, 11), GENES - 2)[:SIG - 2] + 1
    joined = jnp.concatenate([jnp.array([0, GENES - 1], jnp.int32), first.astype(jnp.int32)])
    order = jax.random.permutation(jax.random.fold_in(key, 12), SIG)
    return joined[order].astype(jnp.int32)


def place_ends(result, own_key, smallest, largest):
    shape = result.shape
    place = [jax.random.randint(jax.random.fold_in(own_key, axis), (), 0, shape[axis]) for axis in range(len(shape))]
    result = result.at[tuple(place)].set(smallest)
    longest = shape.index(max(shape))
    place[longest] = (place[longest] + 1) % shape[longest]
    return result.at[tuple(place)].set(largest)


def shard_levels(rng, dims, pieces, smallest, high):
    gain = 1.0
    for position, blocks in pieces:
        heights = jax.random.uniform(jax.random.fold_in(jax.random.fold_in(rng, 6), position), (blocks,), jnp.float32, smallest / len(pieces), high / len(pieces))
        gain = gain * jnp.repeat(jnp.exp(heights), dims[position] // blocks).reshape((-1,) + (1,) * (len(dims) - 1 - position))
    return gain


def normal_values(own_key, extent, width, reach, shards=(), kind=jnp.bfloat16):
    result = jax.random.normal(own_key, extent, jnp.float32) * width
    if len(shards) > 0:
        result = shard_levels(own_key, extent, shards, -0.22, 0.18) * result
    return jnp.clip(result, min=-reach, max=reach).astype(kind)


def setup_inputs(seed: int = 0) -> dict:
    seeds = jax.random.split(jax.random.key(seed), 5)
    return {
        "expression": normal_values(seeds[0], (SAMPLES, GENES), 1.0, 6.0, ((0, 2), (1, 4))),
        "profile": normal_values(seeds[1], (GENES, K), SIG ** -0.5, 0.25, ((0, 4),), jnp.float32),
        "dosage": place_ends(jax.random.randint(seeds[2], (SAMPLES, VARIANTS), 0, 3), jax.random.fold_in(seeds[2], 1), 0, 2).astype(jnp.int32),
        "signature": draw_signature(jax.random.fold_in(seeds[4], 71), 0),
    }


def chol_solve(gram, rhs):
    factor = jnp.linalg.cholesky(gram)
    return jax.scipy.linalg.cho_solve((factor, True), rhs)

def reference(expression, profile, dosage, signature):
    high = lax.Precision.HIGHEST
    member = jnp.zeros((GENES,), jnp.float32).at[signature].set(1.0)
    masked = profile * member[:, None]
    gram = jnp.dot(masked.T, masked, precision=high)
    floats = expression.astype(jnp.float32)
    rhs = jnp.dot(masked.T, floats.T, precision=high)
    props_t = chol_solve(gram, rhs)
    props = props_t.T
    pp_mat = jnp.dot(props_t, props, precision=high)
    py_mat = jnp.dot(props_t, floats, precision=high)
    coef = chol_solve(pp_mat, py_mat)
    rounded = props.astype(jnp.bfloat16).astype(jnp.float32)
    dos_float = dosage.astype(jnp.float32)
    weights = (rounded[:, :, None] * props[:, None, :]).reshape(SAMPLES, K * K)

    def block(index):
        piece = lax.dynamic_slice_in_dim(dos_float, (index * V_DEV).astype(jnp.int32), V_DEV, 1)
        design = (piece[:, :, None] * rounded[:, None, :]).reshape(SAMPLES, V_DEV * K)
        cross = jnp.dot(design.T, floats, precision=high)
        corr = jnp.dot(piece.T, weights, precision=high).reshape(V_DEV * K, K)
        return cross - jnp.dot(corr, coef, precision=high)
    parts = lax.map(block, jnp.arange(N_VARIANT, dtype=jnp.int32))
    scale = jnp.float32(1.0 / math.sqrt(SAMPLES))
    interaction = parts.reshape(VARIANTS * K, GENES) * scale
    return (interaction, props)
```

```python
import functools
import math

import jax
import jax.numpy as jnp
from jax import lax
from jax.experimental import pallas as pl
from jax.experimental.pallas import tpu as pltpu
from jax.sharding import PartitionSpec as P

F32 = jnp.float32
BF16 = jnp.bfloat16
VMEM_LIMIT = 32 << 20
LANES = 128
ROWS = 8


def round_up(n, m):
    return (n + m - 1) // m * m


def in_hbm(x):
    return pltpu.with_memory_space_constraint(x, pltpu.HBM)


def split3(x):
    hi = x.astype(BF16).astype(F32)
    rest = x - hi
    mid = rest.astype(BF16).astype(F32)
    return hi, mid, rest - mid


def stacked(parts, rows):
    have = sum(p.shape[0] for p in parts)
    if have < rows:
        parts = list(parts) + [jnp.zeros((rows - have, parts[0].shape[1]), F32)]
    return jnp.concatenate(parts, axis=0).astype(BF16)


def put(index_row, index_col, values, shape):
    row = lax.broadcasted_iota(jnp.int32, shape, 0)
    col = lax.broadcasted_iota(jnp.int32, shape, 1)
    out = jnp.zeros(shape, F32)
    for (i, j), value in values.items():
        hit = (col == j) if i is None else ((row == i) & (col == j))
        out = jnp.where(hit, value, out)
    return out


def cholesky(entry, n):
    low = {}
    inv = []
    for j in range(n):
        d = entry(j, j)
        for k in range(j):
            d = d - low[j, k] * low[j, k]
        root = jnp.sqrt(d)
        low[j, j] = root
        inv.append(1.0 / root)
        for i in range(j + 1, n):
            v = entry(i, j)
            for k in range(j):
                v = v - low[i, k] * low[j, k]
            low[i, j] = v * inv[j]
    return low, inv


def substitute(low, inv, right):
    n = len(right)
    y = []
    for i in range(n):
        v = right[i]
        for k in range(i):
            v = v - low[i, k] * y[k]
        y.append(v * inv[i])
    x = [None] * n
    for i in reversed(range(n)):
        v = y[i]
        for k in range(i + 1, n):
            v = v - low[k, i] * x[k]
        x[i] = v * inv[i]
    return x


def entries(tile):
    cache = {}

    def entry(i, j):
        if (i, j) not in cache:
            cache[i, j] = jnp.broadcast_to(tile[i : i + 1, j : j + 1], (ROWS, LANES))
        return cache[i, j]

    return entry


def wide(tile, like):
    rows, cols = like
    if rows == 1:
        return jnp.concatenate([tile[0:1]] * (cols // LANES), axis=1)
    return jnp.concatenate([tile] * (rows // ROWS), axis=0)


def rhs_kernel(
    types, pieces, signature_in, profile_in, expression, held, parts, signature, profile, sems, few
):
    samples, genes = expression.shape
    step = samples // pieces
    copies = []
    early = [
        pltpu.make_async_copy(signature_in, signature, few.at[0]),
        pltpu.make_async_copy(profile_in, profile, few.at[1]),
    ]
    for copy in early:
        copy.start()
    for i in range(pieces):
        rows = pl.ds(i * step, step)
        copy = pltpu.make_async_copy(expression.at[rows], held.at[rows], sems.at[i])
        copy.start()
        copies.append(copy)

    for copy in early:
        copy.wait()
    groups = genes // LANES
    base = lax.axis_index("gene") * genes
    shape = (groups, LANES)
    ids = (
        base
        + lax.broadcasted_iota(jnp.int32, shape, 0) * LANES
        + lax.broadcasted_iota(jnp.int32, shape, 1)
    )

    n_sig = signature.shape[0]
    unroll = 10 if n_sig % 10 == 0 else 1

    def look(i, member):
        for u in range(unroll):
            member = member | (ids == signature[i * unroll + u]).astype(jnp.int32)
        return member

    member = lax.fori_loop(0, n_sig // unroll, look, jnp.zeros(shape, jnp.int32))
    member = (member > 0).astype(F32)
    row = jnp.concatenate([member[h : h + 1] for h in range(groups)], axis=1)
    masked = profile[...] * row
    masked = jnp.concatenate([masked, jnp.zeros((ROWS - types, genes), F32)], axis=0)
    left = stacked(split3(masked), 32)

    gram = {}
    for j in range(types):
        gram[None, j] = jnp.sum(masked * masked[j : j + 1], axis=1, keepdims=True)
    parts[types * samples // LANES :, :] = put(None, None, gram, (ROWS, LANES))

    for i in range(pieces):
        copies[i].wait()
        out = lax.dot_general(
            left,
            held[i * step : (i + 1) * step, :],
            (((1,), (1,)), ((), ())),
            preferred_element_type=F32,
        )
        out = out[0:ROWS] + (out[ROWS : 2 * ROWS] + out[2 * ROWS : 3 * ROWS])
        for c in range(step // LANES):
            at = (i * step // LANES + c) * types
            parts[at : at + types, :] = out[:types, c * LANES : (c + 1) * LANES]


def right_sides(expression, profile_t, signature):
    samples, genes = expression.shape
    types = profile_t.shape[0]
    pieces = 8
    rows = types * samples // LANES + ROWS
    return pl.pallas_call(
        functools.partial(rhs_kernel, types, pieces),
        in_specs=[pl.BlockSpec(memory_space=pltpu.HBM)] * 3,
        out_specs=[pl.BlockSpec(memory_space=pltpu.VMEM)] * 2,
        out_shape=[
            pltpu.VMEM((samples, genes), BF16),
            jax.ShapeDtypeStruct((rows, LANES), F32),
        ],
        scratch_shapes=[
            pltpu.SMEM(signature.shape, jnp.int32),
            pltpu.VMEM(profile_t.shape, F32),
            pltpu.SemaphoreType.DMA((pieces,)),
            pltpu.SemaphoreType.DMA((2,)),
        ],
        compiler_params=pltpu.CompilerParams(vmem_limit_bytes=VMEM_LIMIT),
        cost_estimate=pl.CostEstimate(
            flops=2 * 32 * samples * genes, bytes_accessed=2 * samples * genes, transcendentals=0
        ),
        name="right_sides",
    )(in_hbm(signature), in_hbm(profile_t), in_hbm(expression))


def dosage_kernel(own, dosage, first, rest):
    block, variants = dosage.shape
    wide_d = dosage[...].astype(F32)
    if own < variants:
        place = lax.axis_index("sample") * own
        wide_d = pltpu.roll(wide_d, lax.rem(variants - place, variants), 1)
    turned = wide_d.T
    pad = first.shape[0] - own
    mine = turned[:own]
    if pad:
        mine = jnp.concatenate([mine, jnp.zeros((pad, block), F32)], axis=0)
    first[...] = mine.astype(BF16)
    left = variants - own
    if left:
        others = turned[own:]
        pad = rest.shape[0] - left
        if pad:
            others = jnp.concatenate([others, jnp.zeros((pad, block), F32)], axis=0)
        rest[...] = others.astype(BF16)


def turn_dosage(dosage, own):
    samples, variants = dosage.shape
    block = 512
    first, rest = round_up(own, 16), round_up(variants - own, 16)
    return pl.pallas_call(
        functools.partial(dosage_kernel, own),
        grid=(samples // block,),
        in_specs=[pl.BlockSpec((block, variants), lambda i: (i, 0))],
        out_specs=[
            pl.BlockSpec((first, block), lambda i: (0, i)),
            pl.BlockSpec((rest, block), lambda i: (0, i)),
        ],
        out_shape=[
            jax.ShapeDtypeStruct((first, samples), BF16),
            jax.ShapeDtypeStruct((rest, samples), BF16),
        ],
        compiler_params=pltpu.CompilerParams(vmem_limit_bytes=VMEM_LIMIT),
        cost_estimate=pl.CostEstimate(
            flops=samples * variants, bytes_accessed=6 * samples * variants, transcendentals=0
        ),
        name="turn_dosage",
    )(in_hbm(dosage))


def design_rows(left, dosage, rounded, cols, count):
    types = len(rounded)
    width = rounded[0].shape[1]
    for k in range(types):
        spread = jnp.broadcast_to(rounded[k], (16, width)).astype(BF16)
        for q in range(count // 16):
            at = k * count + q * 16
            left[at : at + 16, :] = dosage[q * 16 : q * 16 + 16, cols] * spread


def first_kernel(
    types, step, own_parts, *refs
):
    (x_parts, y_parts, d_parts, mine, others, held, cross, props, kept, small, corr_own, corr_oth, left, weights, packed) = refs
    samples, genes = held.shape
    groups = samples // LANES
    last = types * groups
    n_mine, n_others = mine.shape[0], others.shape[0]

    def total(rows):
        return (own_parts[rows, :] + x_parts[rows, :]) + (y_parts[rows, :] + d_parts[rows, :])

    gram = total(slice(last, last + ROWS))
    low, inv = cholesky(entries(gram), types)
    like = (groups, LANES)
    low = {key: wide(value, like) for key, value in low.items() if key[0] != key[1]}
    inv = [wide(value, like) for value in inv]
    right = [total(pl.ds(k, groups, stride=types)) for k in range(types)]
    solved = substitute(low, inv, right)

    pp = {}
    for i in range(types):
        for j in range(i, types):
            value = jnp.sum(solved[i] * solved[j], axis=(0, 1), keepdims=True)
            pp[i, j] = value
            pp[j, i] = value
    small[ROWS:, :] = jnp.concatenate(
        [put(None, None, pp, (ROWS, LANES)), jnp.zeros((ROWS, genes - LANES), F32)], axis=1
    )

    for k in range(types):
        packed[pl.ds(k, groups, stride=ROWS), :] = solved[k]
    packed[pl.ds(types, groups, stride=ROWS), :] = jnp.zeros(like, F32)

    n_rows = types * n_others
    for c in range(samples // step):
        cols = slice(c * step, (c + 1) * step)
        at = c * step // LANES * ROWS
        p = jnp.concatenate(
            [packed[at + g * ROWS : at + (g + 1) * ROWS, :] for g in range(step // LANES)], axis=1
        )
        props[:, cols] = p[:types]
        pieces = split3(p)
        kept[:, cols] = pieces[0]
        rounded = [pieces[0][k : k + 1] for k in range(types)]
        design_rows(left, others, rounded, cols, n_others)
        left[n_rows:, :] = stacked(pieces, 32)
        w = jnp.concatenate([r * p for r in rounded], axis=0)
        w_parts = split3(w)
        span = ROWS * types
        for s in range(3):
            weights[s * 64 : s * 64 + 64, :] = stacked([w_parts[s]], 64)
        out = jnp.dot(left[...], held[cols, :], preferred_element_type=F32)
        contract = (((1,), (1,)), ((), ()))
        co = lax.dot_general(others[:, cols], weights[...], contract, preferred_element_type=F32)
        cm = lax.dot_general(mine[:, cols], weights[...], contract, preferred_element_type=F32)
        extra = out[n_rows : n_rows + ROWS] + (
            out[n_rows + ROWS : n_rows + 2 * ROWS] + out[n_rows + 2 * ROWS : n_rows + 3 * ROWS]
        )
        if c == 0:
            cross[...] = out[:n_rows]
            small[:ROWS, :] = extra
            corr_oth[...] = co
            corr_own[...] = cm
        else:
            cross[...] += out[:n_rows]
            small[:ROWS, :] += extra
            corr_oth[...] += co
            corr_own[...] += cm


def first_products(parts, mine, others, held, types):
    samples, genes = held.shape
    step = 512
    n_mine, n_others = mine.shape[0], others.shape[0]
    vmem = pl.BlockSpec(memory_space=pltpu.VMEM)
    return pl.pallas_call(
        functools.partial(first_kernel, types, step),
        in_specs=[vmem] * 7,
        out_specs=[vmem] * 6,
        out_shape=[
            jax.ShapeDtypeStruct((types * n_others, genes), F32),
            jax.ShapeDtypeStruct((types, samples), F32),
            pltpu.VMEM((ROWS, samples), F32),
            jax.ShapeDtypeStruct((2 * ROWS, genes), F32),
            jax.ShapeDtypeStruct((n_mine, 192), F32),
            jax.ShapeDtypeStruct((n_others, 192), F32),
        ],
        scratch_shapes=[
            pltpu.VMEM((types * n_others + 32, step), BF16),
            pltpu.VMEM((192, step), BF16),
            pltpu.VMEM((samples // LANES * ROWS, LANES), F32),
        ],
        compiler_params=pltpu.CompilerParams(vmem_limit_bytes=VMEM_LIMIT),
        cost_estimate=pl.CostEstimate(
            flops=2 * types * n_others * samples * genes,
            bytes_accessed=2 * samples * genes,
            transcendentals=0,
        ),
        name="first_products",
    )(*parts, mine, others, held)


def second_kernel(types, step, kept, mine, held, cross, left):
    samples = held.shape[0]
    n_mine = mine.shape[0]
    for c in range(samples // step):
        cols = slice(c * step, (c + 1) * step)
        p = kept[:, cols]
        design_rows(left, mine, [p[k : k + 1] for k in range(types)], cols, n_mine)
        out = jnp.dot(left[...], held[cols, :], preferred_element_type=F32)
        if c == 0:
            cross[...] = out
        else:
            cross[...] += out


def second_products(kept, mine, held, types):
    samples, genes = held.shape
    step = 512
    rows = types * mine.shape[0]
    vmem = pl.BlockSpec(memory_space=pltpu.VMEM)
    return pl.pallas_call(
        functools.partial(second_kernel, types, step),
        in_specs=[vmem] * 3,
        out_specs=vmem,
        out_shape=jax.ShapeDtypeStruct((rows, genes), F32),
        scratch_shapes=[pltpu.VMEM((rows, step), BF16)],
        compiler_params=pltpu.CompilerParams(vmem_limit_bytes=VMEM_LIMIT),
        cost_estimate=pl.CostEstimate(
            flops=2 * rows * samples * genes, bytes_accessed=2 * samples * genes, transcendentals=0
        ),
        name="second_products",
    )(kept, mine, held)


def last_kernel(types, scale, own, peers, *refs):
    cross_own, small_own, corr_own = refs[:3]
    rest = refs[3 : 3 + 3 * peers]
    out, turned, ready, sems = refs[3 + 3 * peers :]
    n_mine = corr_own.shape[0]
    genes = cross_own.shape[1]

    small = small_own[...]
    corr = corr_own[...]
    for i in range(peers):
        small = small + rest[3 * i + 1][...]
        corr = corr + rest[3 * i + 2][...]
    corr = corr[:, 0:64] + (corr[:, 64:128] + corr[:, 128:192])
    corr_t = corr.T
    low, inv = cholesky(entries(small[ROWS:, :LANES]), types)
    like = (1, genes)
    low = {key: wide(value, like) for key, value in low.items() if key[0] != key[1]}
    inv = [wide(value, like) for value in inv]
    coef = substitute(low, inv, [small[k : k + 1] for k in range(types)])
    coef = jnp.concatenate(coef + [jnp.zeros((ROWS - types, genes), F32)], axis=0)
    q = split3(coef)
    right = stacked([q[0], q[1], q[2], q[0], q[1], q[0]], 48)
    for k in range(types):
        c = split3(corr_t[ROWS * k : ROWS * (k + 1)])
        turned[:, k * n_mine : (k + 1) * n_mine] = jnp.concatenate(
            [c[0], c[0], c[0], c[1], c[1], c[2]], axis=0
        )
    turned_b = turned[...].astype(BF16)
    copies = []
    for t in range(genes // LANES):
        lanes = slice(t * LANES, (t + 1) * LANES)
        fitted = lax.dot_general(
            turned_b, right[:, lanes], (((0,), (0,)), ((), ())), preferred_element_type=F32
        )
        for k in range(types):
            rows = slice(k * n_mine, k * n_mine + own)
            value = cross_own[rows, lanes]
            for i in range(peers):
                value = value + rest[3 * i][k * own : (k + 1) * own, lanes]
            ready[t, pl.ds(k, own, stride=types), :] = (value - fitted[rows]) * scale
        copy = pltpu.make_async_copy(ready.at[t], out.at[:, pl.ds(t * LANES, LANES)], sems.at[t])
        copy.start()
        copies.append(copy)
    for copy in copies:
        copy.wait()


def finish(cross, small, corr, received, own, types, scale):
    genes = cross.shape[1]
    n_mine = corr.shape[0]
    vmem = pl.BlockSpec(memory_space=pltpu.VMEM)
    flat = [piece for group in received for piece in group]
    return pl.pallas_call(
        functools.partial(last_kernel, types, scale, own, len(received)),
        in_specs=[vmem] * (3 + len(flat)),
        out_specs=pl.BlockSpec(memory_space=pl.ANY),
        out_shape=jax.ShapeDtypeStruct((types * own, genes), F32),
        scratch_shapes=[
            pltpu.VMEM((48, types * n_mine), F32),
            pltpu.VMEM((genes // LANES, types * own, LANES), F32),
            pltpu.SemaphoreType.DMA((genes // LANES,)),
        ],
        compiler_params=pltpu.CompilerParams(vmem_limit_bytes=VMEM_LIMIT),
        name="finish",
    )(cross, small, corr, *flat)


def exchange_all(part, n_gene):
    def swap(offset):
        return lax.ppermute(part, "gene", [(i, i ^ offset) for i in range(n_gene)])

    return (part, swap(1), swap(2), swap(3))


def local(n_gene, n_sample, expression, profile, dosage, signature):
    s_dev, g_dev = expression.shape
    v_dev = dosage.shape[1]
    types = profile.shape[1]
    own = v_dev // n_sample
    scale = 1.0 / math.sqrt(s_dev * n_sample)

    held, part = right_sides(expression, profile.T, signature)
    mine, others = turn_dosage(dosage, own)
    parts = exchange_all(part, n_gene)
    cross_oth, props, kept, small, corr_own, corr_oth = first_products(
        parts, mine, others, held, types
    )
    received = []
    n_mine, n_oth = mine.shape[0], others.shape[0]
    for d in range(1, n_sample):
        pairs = [(i, (i + d) % n_sample) for i in range(n_sample)]
        cross, corr = cross_oth, corr_oth
        if n_oth != own:
            cut = slice((d - 1) * own, d * own)
            cross = cross.reshape(types, n_oth, g_dev)[:, cut].reshape(types * own, g_dev)
            corr = jnp.pad(corr[cut], ((0, n_mine - own), (0, 0)))
        received.append([lax.ppermute(x, "sample", pairs) for x in (cross, small, corr)])
    cross_own = second_products(kept, mine, held, types)
    interaction = finish(cross_own, small, corr_own, received, own, types, scale)
    return interaction, props.T


def solution(mesh):
    placed = (P("sample", "gene"), P("gene", None), P("sample", "variant"), P())
    return jax.shard_map(
        functools.partial(local, mesh.shape["gene"], mesh.shape["sample"]),
        mesh=mesh,
        in_specs=placed,
        out_specs=(P(("variant", "sample"), "gene"), P("sample", None)),
        check_vma=False,
    )
```

```python
import functools
import math

import jax
import jax.numpy as jnp
from jax import lax
from jax.experimental import pallas as pl
from jax.experimental.pallas import tpu as pltpu
from jax.sharding import PartitionSpec as P

F32 = jnp.float32
BF16 = jnp.bfloat16
VMEM_LIMIT = 32 << 20
LANES = 128
ROWS = 8


def round_up(n, m):
    return (n + m - 1) // m * m


def in_hbm(x):
    return pltpu.with_memory_space_constraint(x, pltpu.HBM)


def split3(x):
    hi = x.astype(BF16).astype(F32)
    rest = x - hi
    mid = rest.astype(BF16).astype(F32)
    return hi, mid, rest - mid


def stacked(parts, rows):
    have = sum(p.shape[0] for p in parts)
    if have < rows:
        parts = list(parts) + [jnp.zeros((rows - have, parts[0].shape[1]), F32)]
    return jnp.concatenate(parts, axis=0).astype(BF16)


def put(index_row, index_col, values, shape):
    row = lax.broadcasted_iota(jnp.int32, shape, 0)
    col = lax.broadcasted_iota(jnp.int32, shape, 1)
    out = jnp.zeros(shape, F32)
    for (i, j), value in values.items():
        hit = (col == j) if i is None else ((row == i) & (col == j))
        out = jnp.where(hit, value, out)
    return out


def cholesky(entry, n):
    low = {}
    inv = []
    for j in range(n):
        d = entry(j, j)
        for k in range(j):
            d = d - low[j, k] * low[j, k]
        root = lax.rsqrt(d)
        root = root * (1.5 - 0.5 * d * root * root)
        inv.append(root)
        for i in range(j + 1, n):
            v = entry(i, j)
            for k in range(j):
                v = v - low[i, k] * low[j, k]
            low[i, j] = v * root
    return low, inv


def substitute(low, inv, right):
    n = len(right)
    y = []
    for i in range(n):
        v = right[i]
        for k in range(i):
            v = v - low[i, k] * y[k]
        y.append(v * inv[i])
    x = [None] * n
    for i in reversed(range(n)):
        v = y[i]
        for k in range(i + 1, n):
            v = v - low[k, i] * x[k]
        x[i] = v * inv[i]
    return x


def entries(tile):
    cache = {}

    def entry(i, j):
        if (i, j) not in cache:
            cache[i, j] = jnp.broadcast_to(tile[i : i + 1, j : j + 1], (ROWS, LANES))
        return cache[i, j]

    return entry


def wide(tile, like):
    rows, cols = like
    if rows == 1:
        return jnp.concatenate([tile[0:1]] * (cols // LANES), axis=1)
    return jnp.concatenate([tile] * (rows // ROWS), axis=0)


def rhs_kernel(
    types, pieces, signature_in, profile_in, expression, held, parts, signature, profile, sems, few
):
    samples, genes = expression.shape
    step = samples // pieces
    copies = []
    early = [
        pltpu.make_async_copy(signature_in, signature, few.at[0]),
        pltpu.make_async_copy(profile_in, profile, few.at[1]),
    ]
    for copy in early:
        copy.start()
    for i in range(pieces):
        rows = pl.ds(i * step, step)
        copy = pltpu.make_async_copy(expression.at[rows], held.at[rows], sems.at[i])
        copy.start()
        copies.append(copy)

    for copy in early:
        copy.wait()
    groups = genes // LANES
    base = lax.axis_index("gene") * genes
    shape = (groups, LANES)
    ids = (
        base
        + lax.broadcasted_iota(jnp.int32, shape, 0) * LANES
        + lax.broadcasted_iota(jnp.int32, shape, 1)
    )

    n_sig = signature.shape[0]
    unroll = 10 if n_sig % 10 == 0 else 1

    def look(i, member):
        for u in range(unroll):
            member = member | (ids == signature[i * unroll + u]).astype(jnp.int32)
        return member

    member = lax.fori_loop(0, n_sig // unroll, look, jnp.zeros(shape, jnp.int32))
    member = (member > 0).astype(F32)
    row = jnp.concatenate([member[h : h + 1] for h in range(groups)], axis=1)
    masked = profile[...] * row
    masked = jnp.concatenate([masked, jnp.zeros((ROWS - types, genes), F32)], axis=0)
    left = stacked(split3(masked), 32)

    gram = {}
    for j in range(types):
        gram[None, j] = jnp.sum(masked * masked[j : j + 1], axis=1, keepdims=True)
    parts[types * samples // LANES :, :] = put(None, None, gram, (ROWS, LANES))

    for i in range(pieces):
        copies[i].wait()
        out = lax.dot_general(
            left,
            held[i * step : (i + 1) * step, :],
            (((1,), (1,)), ((), ())),
            preferred_element_type=F32,
        )
        out = out[0:ROWS] + (out[ROWS : 2 * ROWS] + out[2 * ROWS : 3 * ROWS])
        for c in range(step // LANES):
            at = (i * step // LANES + c) * types
            parts[at : at + types, :] = out[:types, c * LANES : (c + 1) * LANES]


def right_sides(expression, profile_t, signature):
    samples, genes = expression.shape
    types = profile_t.shape[0]
    pieces = 2
    rows = types * samples // LANES + ROWS
    return pl.pallas_call(
        functools.partial(rhs_kernel, types, pieces),
        in_specs=[pl.BlockSpec(memory_space=pltpu.HBM)] * 3,
        out_specs=[pl.BlockSpec(memory_space=pltpu.VMEM)] * 2,
        out_shape=[
            pltpu.VMEM((samples, genes), BF16),
            jax.ShapeDtypeStruct((rows, LANES), F32),
        ],
        scratch_shapes=[
            pltpu.SMEM(signature.shape, jnp.int32),
            pltpu.VMEM(profile_t.shape, F32),
            pltpu.SemaphoreType.DMA((pieces,)),
            pltpu.SemaphoreType.DMA((2,)),
        ],
        compiler_params=pltpu.CompilerParams(vmem_limit_bytes=VMEM_LIMIT),
        cost_estimate=pl.CostEstimate(
            flops=2 * 32 * samples * genes, bytes_accessed=2 * samples * genes, transcendentals=0
        ),
        name="right_sides",
    )(in_hbm(signature), in_hbm(profile_t), in_hbm(expression))


def dosage_kernel(own, pieces, dosage_in, first, rest, dosage, sems):
    samples, variants = dosage.shape
    step = samples // pieces
    copies = []
    for i in range(pieces):
        rows = pl.ds(i * step, step)
        copy = pltpu.make_async_copy(dosage_in.at[rows], dosage.at[rows], sems.at[i])
        copy.start()
        copies.append(copy)
    shift = lax.rem(variants - lax.axis_index("sample") * own, variants)
    for i in range(pieces):
        copies[i].wait()
        cols = slice(i * step, (i + 1) * step)
        turned = pltpu.roll(dosage[cols, :].astype(F32), shift, 1).T
        first[:, cols] = stacked([turned[:own]], first.shape[0])
        rest[:, cols] = stacked([turned[own:]], rest.shape[0])


def turn_dosage(dosage, own):
    samples, variants = dosage.shape
    pieces = 4
    first, rest = round_up(own, 16), round_up(variants - own, 16)
    return pl.pallas_call(
        functools.partial(dosage_kernel, own, pieces),
        in_specs=[pl.BlockSpec(memory_space=pltpu.HBM)],
        out_specs=[pl.BlockSpec(memory_space=pltpu.VMEM)] * 2,
        out_shape=[
            pltpu.VMEM((first, samples), BF16),
            pltpu.VMEM((rest, samples), BF16),
        ],
        scratch_shapes=[
            pltpu.VMEM(dosage.shape, jnp.int32),
            pltpu.SemaphoreType.DMA((pieces,)),
        ],
        compiler_params=pltpu.CompilerParams(vmem_limit_bytes=VMEM_LIMIT),
        cost_estimate=pl.CostEstimate(
            flops=samples * variants, bytes_accessed=6 * samples * variants, transcendentals=0
        ),
        name="turn_dosage",
    )(in_hbm(dosage))


def design_rows(left, dosage, rounded, cols, count):
    types = len(rounded)
    width = rounded[0].shape[1]
    for k in range(types):
        spread = jnp.broadcast_to(rounded[k], (16, width)).astype(BF16)
        for q in range(count // 16):
            at = k * count + q * 16
            left[at : at + 16, :] = dosage[q * 16 : q * 16 + 16, cols] * spread


def first_kernel(
    types, step, own_parts, *refs
):
    (x_parts, y_parts, d_parts, mine, others, held, cross, props, kept, small, corr_own, corr_oth, left, weights, packed) = refs
    samples, genes = held.shape
    groups = samples // LANES
    last = types * groups
    n_mine, n_others = mine.shape[0], others.shape[0]

    def total(rows):
        return (own_parts[rows, :] + x_parts[rows, :]) + (y_parts[rows, :] + d_parts[rows, :])

    gram = total(slice(last, last + ROWS))
    low, inv = cholesky(entries(gram), types)
    like = (groups, LANES)
    low = {key: wide(value, like) for key, value in low.items()}
    inv = [wide(value, like) for value in inv]
    right = [total(pl.ds(k, groups, stride=types)) for k in range(types)]
    solved = substitute(low, inv, right)

    pp = {}
    for i in range(types):
        for j in range(i, types):
            value = jnp.sum(solved[i] * solved[j], axis=(0, 1), keepdims=True)
            pp[i, j] = value
            pp[j, i] = value
    small[ROWS:, :] = jnp.concatenate(
        [put(None, None, pp, (ROWS, LANES)), jnp.zeros((ROWS, genes - LANES), F32)], axis=1
    )

    for k in range(types):
        packed[pl.ds(k, groups, stride=ROWS), :] = solved[k]
    packed[pl.ds(types, groups, stride=ROWS), :] = jnp.zeros(like, F32)

    n_rows = types * n_others
    for c in range(samples // step):
        cols = slice(c * step, (c + 1) * step)
        at = c * step // LANES * ROWS
        p = jnp.concatenate(
            [packed[at + g * ROWS : at + (g + 1) * ROWS, :] for g in range(step // LANES)], axis=1
        )
        props[:, cols] = p[:types]
        pieces = split3(p)
        kept[:, cols] = pieces[0]
        rounded = [pieces[0][k : k + 1] for k in range(types)]
        design_rows(left, others, rounded, cols, n_others)
        left[n_rows:, :] = stacked(pieces, 32)
        w = jnp.concatenate([r * p for r in rounded], axis=0)
        w_parts = split3(w)
        span = ROWS * types
        for s in range(3):
            weights[s * 64 : s * 64 + 64, :] = stacked([w_parts[s]], 64)
        out = jnp.dot(left[...], held[cols, :], preferred_element_type=F32)
        contract = (((1,), (1,)), ((), ()))
        co = lax.dot_general(others[:, cols], weights[...], contract, preferred_element_type=F32)
        cm = lax.dot_general(mine[:, cols], weights[...], contract, preferred_element_type=F32)
        extra = out[n_rows : n_rows + ROWS] + (
            out[n_rows + ROWS : n_rows + 2 * ROWS] + out[n_rows + 2 * ROWS : n_rows + 3 * ROWS]
        )
        if c == 0:
            cross[...] = out[:n_rows]
            small[:ROWS, :] = extra
            corr_oth[...] = co
            corr_own[...] = cm
        else:
            cross[...] += out[:n_rows]
            small[:ROWS, :] += extra
            corr_oth[...] += co
            corr_own[...] += cm


def first_products(parts, mine, others, held, types):
    samples, genes = held.shape
    step = 512
    n_mine, n_others = mine.shape[0], others.shape[0]
    vmem = pl.BlockSpec(memory_space=pltpu.VMEM)
    return pl.pallas_call(
        functools.partial(first_kernel, types, step),
        in_specs=[vmem] * 7,
        out_specs=[vmem] * 6,
        out_shape=[
            jax.ShapeDtypeStruct((types * n_others, genes), F32),
            jax.ShapeDtypeStruct((types, samples), F32),
            pltpu.VMEM((ROWS, samples), F32),
            jax.ShapeDtypeStruct((2 * ROWS, genes), F32),
            jax.ShapeDtypeStruct((n_mine, 192), F32),
            jax.ShapeDtypeStruct((n_others, 192), F32),
        ],
        scratch_shapes=[
            pltpu.VMEM((types * n_others + 32, step), BF16),
            pltpu.VMEM((192, step), BF16),
            pltpu.VMEM((samples // LANES * ROWS, LANES), F32),
        ],
        compiler_params=pltpu.CompilerParams(vmem_limit_bytes=VMEM_LIMIT),
        cost_estimate=pl.CostEstimate(
            flops=2 * types * n_others * samples * genes,
            bytes_accessed=2 * samples * genes,
            transcendentals=0,
        ),
        name="first_products",
    )(*parts, mine, others, held)


def second_kernel(types, step, kept, mine, held, cross, left):
    samples = held.shape[0]
    n_mine = mine.shape[0]
    for c in range(samples // step):
        cols = slice(c * step, (c + 1) * step)
        p = kept[:, cols]
        design_rows(left, mine, [p[k : k + 1] for k in range(types)], cols, n_mine)
        out = jnp.dot(left[...], held[cols, :], preferred_element_type=F32)
        if c == 0:
            cross[...] = out
        else:
            cross[...] += out


def second_products(kept, mine, held, types):
    samples, genes = held.shape
    step = 512
    rows = types * mine.shape[0]
    vmem = pl.BlockSpec(memory_space=pltpu.VMEM)
    return pl.pallas_call(
        functools.partial(second_kernel, types, step),
        in_specs=[vmem] * 3,
        out_specs=vmem,
        out_shape=jax.ShapeDtypeStruct((rows, genes), F32),
        scratch_shapes=[pltpu.VMEM((rows, step), BF16)],
        compiler_params=pltpu.CompilerParams(vmem_limit_bytes=VMEM_LIMIT),
        cost_estimate=pl.CostEstimate(
            flops=2 * rows * samples * genes, bytes_accessed=2 * samples * genes, transcendentals=0
        ),
        name="second_products",
    )(kept, mine, held)


def last_kernel(types, scale, own, peers, *refs):
    cross_own, small_own, corr_own = refs[:3]
    rest = refs[3 : 3 + 3 * peers]
    out, turned, ready, sems = refs[3 + 3 * peers :]
    n_mine = corr_own.shape[0]
    genes = cross_own.shape[1]

    small = small_own[...]
    corr = corr_own[...]
    for i in range(peers):
        small = small + rest[3 * i + 1][...]
        corr = corr + rest[3 * i + 2][...]
    corr = corr[:, 0:64] + (corr[:, 64:128] + corr[:, 128:192])
    corr_t = corr.T
    low, inv = cholesky(entries(small[ROWS:, :LANES]), types)
    like = (1, genes)
    low = {key: wide(value, like) for key, value in low.items()}
    inv = [wide(value, like) for value in inv]
    coef = substitute(low, inv, [small[k : k + 1] for k in range(types)])
    coef = jnp.concatenate(coef + [jnp.zeros((ROWS - types, genes), F32)], axis=0)
    q = split3(coef)
    right = stacked([q[0], q[1], q[2], q[0], q[1], q[0]], 48)
    for k in range(types):
        c = split3(corr_t[ROWS * k : ROWS * (k + 1)])
        turned[:, k * n_mine : (k + 1) * n_mine] = jnp.concatenate(
            [c[0], c[0], c[0], c[1], c[1], c[2]], axis=0
        )
    turned_b = turned[...].astype(BF16)
    copies = []
    for t in range(genes // LANES):
        lanes = slice(t * LANES, (t + 1) * LANES)
        fitted = lax.dot_general(
            turned_b, right[:, lanes], (((0,), (0,)), ((), ())), preferred_element_type=F32
        )
        for k in range(types):
            rows = slice(k * n_mine, k * n_mine + own)
            value = cross_own[rows, lanes]
            for i in range(peers):
                value = value + rest[3 * i][k * own : (k + 1) * own, lanes]
            ready[t, pl.ds(k, own, stride=types), :] = (value - fitted[rows]) * scale
        copy = pltpu.make_async_copy(ready.at[t], out.at[:, pl.ds(t * LANES, LANES)], sems.at[t])
        copy.start()
        copies.append(copy)
    for copy in copies:
        copy.wait()


def finish(cross, small, corr, received, own, types, scale):
    genes = cross.shape[1]
    n_mine = corr.shape[0]
    vmem = pl.BlockSpec(memory_space=pltpu.VMEM)
    flat = [piece for group in received for piece in group]
    return pl.pallas_call(
        functools.partial(last_kernel, types, scale, own, len(received)),
        in_specs=[vmem] * (3 + len(flat)),
        out_specs=pl.BlockSpec(memory_space=pl.ANY),
        out_shape=jax.ShapeDtypeStruct((types * own, genes), F32),
        scratch_shapes=[
            pltpu.VMEM((48, types * n_mine), F32),
            pltpu.VMEM((genes // LANES, types * own, LANES), F32),
            pltpu.SemaphoreType.DMA((genes // LANES,)),
        ],
        compiler_params=pltpu.CompilerParams(vmem_limit_bytes=VMEM_LIMIT),
        name="finish",
    )(cross, small, corr, *flat)


def exchange_all(part, n_gene):
    def swap(offset):
        return lax.ppermute(part, "gene", [(i, i ^ offset) for i in range(n_gene)])

    return (part, swap(1), swap(2), swap(3))


def local(n_gene, n_sample, expression, profile, dosage, signature):
    s_dev, g_dev = expression.shape
    v_dev = dosage.shape[1]
    types = profile.shape[1]
    own = v_dev // n_sample
    scale = 1.0 / math.sqrt(s_dev * n_sample)

    held, part = right_sides(expression, profile.T, signature)
    mine, others = turn_dosage(dosage, own)
    parts = exchange_all(part, n_gene)
    cross_oth, props, kept, small, corr_own, corr_oth = first_products(
        parts, mine, others, held, types
    )
    received = []
    n_mine, n_oth = mine.shape[0], others.shape[0]
    for d in range(1, n_sample):
        pairs = [(i, (i + d) % n_sample) for i in range(n_sample)]
        cross, corr = cross_oth, corr_oth
        if n_oth != own:
            cut = slice((d - 1) * own, d * own)
            cross = cross.reshape(types, n_oth, g_dev)[:, cut].reshape(types * own, g_dev)
            corr = jnp.pad(corr[cut], ((0, n_mine - own), (0, 0)))
        received.append([lax.ppermute(x, "sample", pairs) for x in (cross, small, corr)])
    cross_own = second_products(kept, mine, held, types)
    interaction = finish(cross_own, small, corr_own, received, own, types, scale)
    return interaction, props.T


def solution(mesh):
    placed = (P("sample", "gene"), P("gene", None), P("sample", "variant"), P())
    return jax.shard_map(
        functools.partial(local, mesh.shape["gene"], mesh.shape["sample"]),
        mesh=mesh,
        in_specs=placed,
        out_specs=(P(("variant", "sample"), "gene"), P("sample", None)),
        check_vma=False,
    )
```

```python
import functools
import math

import jax
import jax.numpy as jnp
from jax import lax
from jax.experimental import pallas as pl
from jax.experimental.pallas import tpu as pltpu
from jax.sharding import PartitionSpec as P

F32 = jnp.float32
BF16 = jnp.bfloat16
VMEM_LIMIT = 32 << 20
LANES = 128
ROWS = 8
RHS_PIECES = 2


def round_up(n, m):
    return (n + m - 1) // m * m


def in_hbm(x):
    return pltpu.with_memory_space_constraint(x, pltpu.HBM)


def split3(x):
    hi = x.astype(BF16).astype(F32)
    rest = x - hi
    mid = rest.astype(BF16).astype(F32)
    return hi, mid, rest - mid


def stacked(parts, rows):
    have = sum(p.shape[0] for p in parts)
    if have < rows:
        parts = list(parts) + [jnp.zeros((rows - have, parts[0].shape[1]), F32)]
    return jnp.concatenate(parts, axis=0).astype(BF16)


def cholesky(entry, n):
    low = {}
    inv = []
    for j in range(n):
        d = entry(j, j)
        for k in range(j):
            d = d - low[j, k] * low[j, k]
        root = lax.rsqrt(d)
        root = root * (1.5 - 0.5 * d * root * root)
        inv.append(root)
        for i in range(j + 1, n):
            v = entry(i, j)
            for k in range(j):
                v = v - low[i, k] * low[j, k]
            low[i, j] = v * root
    return low, inv


def substitute(low, inv, right):
    n = len(right)
    y = []
    for i in range(n):
        v = right[i]
        for k in range(i):
            v = v - low[i, k] * y[k]
        y.append(v * inv[i])
    x = [None] * n
    for i in reversed(range(n)):
        v = y[i]
        for k in range(i + 1, n):
            v = v - low[k, i] * x[k]
        x[i] = v * inv[i]
    return x


def entries(tile):
    cache = {}

    def entry(i, j):
        if (i, j) not in cache:
            cache[i, j] = jnp.broadcast_to(tile[i : i + 1, j : j + 1], (ROWS, LANES))
        return cache[i, j]

    return entry


def inner_products(x, n):
    col = lax.broadcasted_iota(jnp.int32, (ROWS, LANES), 1)
    out = jnp.zeros((ROWS, LANES), F32)
    for j in range(n):
        out = jnp.where(col == j, jnp.sum(x * x[j : j + 1], axis=1, keepdims=True), out)
    return out


def wide(tile, like):
    rows, cols = like
    if rows == 1:
        return jnp.concatenate([tile[0:1]] * (cols // LANES), axis=1)
    return jnp.concatenate([tile] * (rows // ROWS), axis=0)


def rhs_kernel(
    types, halves, pieces, signature_in, profile_in, expression, held, parts, signature, profile, sems, few
):
    samples, genes = held.shape
    step = samples // pieces
    early = [
        pltpu.make_async_copy(signature_in, signature, few.at[0]),
        pltpu.make_async_copy(profile_in, profile, few.at[1]),
    ]
    for copy in early:
        copy.start()
    start = lax.rem(lax.axis_index("variant"), halves) * samples
    copies = []
    for i in range(pieces):
        rows = pl.ds(i * step, step)
        there = pl.ds(pl.multiple_of(start + i * step, step), step)
        copy = pltpu.make_async_copy(expression.at[there], held.at[rows], sems.at[i])
        copy.start()
        copies.append(copy)

    for copy in early:
        copy.wait()
    groups = genes // LANES
    base = lax.axis_index("gene") * genes
    shape = (groups, LANES)
    ids = (
        base
        + lax.broadcasted_iota(jnp.int32, shape, 0) * LANES
        + lax.broadcasted_iota(jnp.int32, shape, 1)
    )

    n_sig = signature.shape[0]
    unroll = 10 if n_sig % 10 == 0 else 1

    def look(i, member):
        for u in range(unroll):
            member = member | (ids == signature[i * unroll + u]).astype(jnp.int32)
        return member

    member = lax.fori_loop(0, n_sig // unroll, look, jnp.zeros(shape, jnp.int32))
    member = (member > 0).astype(F32)
    row = jnp.concatenate([member[h : h + 1] for h in range(groups)], axis=1)
    masked = profile[...] * row
    masked = jnp.concatenate([masked, jnp.zeros((ROWS - types, genes), F32)], axis=0)
    left = stacked(split3(masked), 32)
    parts[types * samples // LANES :, :] = inner_products(masked, types)

    for i in range(pieces):
        copies[i].wait()
        out = lax.dot_general(
            left,
            held[i * step : (i + 1) * step, :],
            (((1,), (1,)), ((), ())),
            preferred_element_type=F32,
        )
        out = out[0:ROWS] + (out[ROWS : 2 * ROWS] + out[2 * ROWS : 3 * ROWS])
        for c in range(step // LANES):
            at = (i * step // LANES + c) * types
            parts[at : at + types, :] = out[:types, c * LANES : (c + 1) * LANES]


def right_sides(expression, profile_t, signature, halves):
    samples, genes = expression.shape
    samples = samples // halves
    types = profile_t.shape[0]
    pieces = RHS_PIECES
    rows = types * samples // LANES + ROWS
    return pl.pallas_call(
        functools.partial(rhs_kernel, types, halves, pieces),
        in_specs=[pl.BlockSpec(memory_space=pltpu.HBM)] * 3,
        out_specs=[pl.BlockSpec(memory_space=pltpu.VMEM)] * 2,
        out_shape=[
            pltpu.VMEM((samples, genes), BF16),
            jax.ShapeDtypeStruct((rows, LANES), F32),
        ],
        scratch_shapes=[
            pltpu.SMEM(signature.shape, jnp.int32),
            pltpu.VMEM(profile_t.shape, F32),
            pltpu.SemaphoreType.DMA((pieces,)),
            pltpu.SemaphoreType.DMA((2,)),
        ],
        compiler_params=pltpu.CompilerParams(vmem_limit_bytes=VMEM_LIMIT),
        cost_estimate=pl.CostEstimate(
            flops=2 * 32 * samples * genes, bytes_accessed=2 * samples * genes, transcendentals=0
        ),
        name="right_sides",
    )(in_hbm(signature), in_hbm(profile_t), in_hbm(expression))


def prepare_kernel(own, halves, pieces, dosage_in, expression, first, rest, *refs):
    held = refs[:-3]
    dosage, sems, far_sem = refs[-3:]
    samples, variants = dosage.shape
    half = samples // halves
    step = samples // pieces
    side = lax.rem(lax.axis_index("variant"), halves)
    copies = []
    for i in range(pieces):
        near = i * step // half
        begin = lax.rem(side + near, halves) * half + (i * step - near * half)
        there = pl.ds(pl.multiple_of(begin, step), step)
        copy = pltpu.make_async_copy(dosage_in.at[there], dosage.at[pl.ds(i * step, step)], sems.at[i])
        copy.start()
        copies.append(copy)
    far = []
    for ref in held:
        there = pl.ds(pl.multiple_of((1 - side) * half, half), half)
        copy = pltpu.make_async_copy(expression.at[there], ref, far_sem)
        copy.start()
        far.append(copy)
    shift = lax.rem(variants - lax.axis_index("sample") * own, variants)
    for i in range(pieces):
        copies[i].wait()
        cols = slice(i * step, (i + 1) * step)
        turned = pltpu.roll(dosage[cols, :].astype(F32), shift, 1).T
        first[:, cols] = stacked([turned[:own]], first.shape[0])
        rest[:, cols] = stacked([turned[own:]], rest.shape[0])
    for copy in far:
        copy.wait()


def prepare(dosage, expression, own, halves):
    samples, variants = dosage.shape
    genes = expression.shape[1]
    pieces = 4
    first, rest = round_up(own, 16), round_up(variants - own, 16)
    return pl.pallas_call(
        functools.partial(prepare_kernel, own, halves, pieces),
        in_specs=[pl.BlockSpec(memory_space=pltpu.HBM)] * 2,
        out_specs=[pl.BlockSpec(memory_space=pltpu.VMEM)] * (1 + halves),
        out_shape=[pltpu.VMEM((first, samples), BF16), pltpu.VMEM((rest, samples), BF16)]
        + [pltpu.VMEM((samples // halves, genes), BF16)] * (halves - 1),
        scratch_shapes=[
            pltpu.VMEM(dosage.shape, jnp.int32),
            pltpu.SemaphoreType.DMA((pieces,)),
            pltpu.SemaphoreType.DMA,
        ],
        compiler_params=pltpu.CompilerParams(vmem_limit_bytes=VMEM_LIMIT),
        cost_estimate=pl.CostEstimate(
            flops=samples * variants, bytes_accessed=6 * samples * variants, transcendentals=0
        ),
        name="prepare",
    )(in_hbm(dosage), in_hbm(expression))


def solve_kernel(types, own_parts, x_parts, y_parts, d_parts, solved, packed):
    groups = (own_parts.shape[0] - ROWS) // types
    last = types * groups

    def total(rows):
        return (own_parts[rows, :] + x_parts[rows, :]) + (y_parts[rows, :] + d_parts[rows, :])

    low, inv = cholesky(entries(total(slice(last, last + ROWS))), types)
    like = (groups, LANES)
    low = {key: wide(value, like) for key, value in low.items()}
    inv = [wide(value, like) for value in inv]
    x = substitute(low, inv, [total(pl.ds(k, groups, stride=types)) for k in range(types)])
    for k in range(types):
        packed[pl.ds(k, groups, stride=ROWS), :] = x[k]
    for k in range(types, ROWS):
        packed[pl.ds(k, groups, stride=ROWS), :] = jnp.zeros(like, F32)
    for g in range(groups):
        solved[:, g * LANES : (g + 1) * LANES] = packed[g * ROWS : (g + 1) * ROWS, :]


def solve(parts, types):
    groups = (parts[0].shape[0] - ROWS) // types
    vmem = pl.BlockSpec(memory_space=pltpu.VMEM)
    return pl.pallas_call(
        functools.partial(solve_kernel, types),
        in_specs=[vmem] * 4,
        out_specs=vmem,
        out_shape=jax.ShapeDtypeStruct((ROWS, groups * LANES), F32),
        scratch_shapes=[pltpu.VMEM((groups * ROWS, LANES), F32)],
        compiler_params=pltpu.CompilerParams(vmem_limit_bytes=VMEM_LIMIT),
        name="solve",
    )(*parts)


def design_rows(left, dosage, rounded, cols, count):
    types = len(rounded)
    width = rounded[0].shape[1]
    for k in range(types):
        spread = jnp.broadcast_to(rounded[k], (16, width)).astype(BF16)
        for q in range(count // 16):
            at = k * count + q * 16
            left[at : at + 16, :] = dosage[q * 16 : q * 16 + 16, cols] * spread


def others_kernel(types, step, first_col, has_before, *refs):
    p_in, mine, others, held = refs[:4]
    before = refs[4:8] if has_before else None
    cross, small, corr_own, corr_oth, left, weights = refs[-6:]
    samples, genes = held.shape
    n_rows = types * others.shape[0]

    pp = inner_products(p_in[...], types)
    small[ROWS:, :] = jnp.concatenate([pp, jnp.zeros((ROWS, genes - LANES), F32)], axis=1)
    if has_before:
        small[ROWS:, :LANES] += before[1][ROWS:, :LANES]

    for c in range(samples // step):
        here = slice(c * step, (c + 1) * step)
        cols = slice(first_col + c * step, first_col + (c + 1) * step)
        p = p_in[:, here]
        pieces = split3(p)
        rounded = [pieces[0][k : k + 1] for k in range(types)]
        design_rows(left, others, rounded, cols, others.shape[0])
        left[n_rows:, :] = stacked(pieces, 32)
        w_parts = split3(jnp.concatenate([r * p for r in rounded], axis=0))
        for s in range(3):
            weights[s * 64 : s * 64 + 64, :] = stacked([w_parts[s]], 64)
        out = jnp.dot(left[...], held[here, :], preferred_element_type=F32)
        contract = (((1,), (1,)), ((), ()))
        co = lax.dot_general(others[:, cols], weights[...], contract, preferred_element_type=F32)
        cm = lax.dot_general(mine[:, cols], weights[...], contract, preferred_element_type=F32)
        py = out[n_rows : n_rows + ROWS] + (
            out[n_rows + ROWS : n_rows + 2 * ROWS] + out[n_rows + 2 * ROWS : n_rows + 3 * ROWS]
        )
        old = None
        if c:
            old = (cross, small, corr_own, corr_oth)
        elif has_before:
            old = before
        if old is None:
            cross[...] = out[:n_rows]
            small[:ROWS, :] = py
            corr_own[...] = cm
            corr_oth[...] = co
        else:
            cross[...] = old[0][...] + out[:n_rows]
            small[:ROWS, :] = old[1][:ROWS, :] + py
            corr_own[...] = old[2][...] + cm
            corr_oth[...] = old[3][...] + co


def others_products(p, mine, others, held, first_col, before, types):
    samples, genes = held.shape
    step = 512
    n_mine, n_others = mine.shape[0], others.shape[0]
    vmem = pl.BlockSpec(memory_space=pltpu.VMEM)
    before = list(before or [])
    return pl.pallas_call(
        functools.partial(others_kernel, types, step, first_col, bool(before)),
        in_specs=[vmem] * (4 + len(before)),
        out_specs=[vmem] * 4,
        out_shape=[
            jax.ShapeDtypeStruct((types * n_others, genes), F32),
            jax.ShapeDtypeStruct((2 * ROWS, genes), F32),
            jax.ShapeDtypeStruct((n_mine, 192), F32),
            jax.ShapeDtypeStruct((n_others, 192), F32),
        ],
        scratch_shapes=[
            pltpu.VMEM((types * n_others + 32, step), BF16),
            pltpu.VMEM((192, step), BF16),
        ],
        compiler_params=pltpu.CompilerParams(vmem_limit_bytes=VMEM_LIMIT),
        cost_estimate=pl.CostEstimate(
            flops=2 * types * n_others * samples * genes,
            bytes_accessed=2 * samples * genes,
            transcendentals=0,
        ),
        name="others_products",
    )(p, mine, others, held, *before)


def own_dot(types, step, p_in, mine, held, lanes, left, add):
    first_col = 0
    first = True
    for p_ref, held_ref in zip(p_in, held):
        samples = held_ref.shape[0]
        for c in range(samples // step):
            here = slice(c * step, (c + 1) * step)
            cols = slice(first_col + c * step, first_col + (c + 1) * step)
            rounded = p_ref[:, here].astype(BF16).astype(F32)
            design_rows(left, mine, [rounded[k : k + 1] for k in range(types)], cols, mine.shape[0])
            add(jnp.dot(left[...], held_ref[here, lanes], preferred_element_type=F32), first)
            first = False
        first_col += samples


def own_kernel(types, step, halves, *refs):
    p_in, held, mine = refs[:halves], refs[halves : 2 * halves], refs[2 * halves]
    cross, props, left = refs[2 * halves + 1 :]
    half = p_in[0].shape[1]
    side = lax.rem(lax.axis_index("variant"), halves)
    for i in range(halves):
        at = pl.multiple_of(lax.rem(side + i, halves) * half, half)
        props[:, pl.ds(at, half)] = p_in[i][:types, :]

    def add(out, first):
        if first:
            cross[...] = out
        else:
            cross[...] += out

    own_dot(types, step, p_in, mine, held, slice(0, cross.shape[1]), left, add)


def own_products(p, mine, held, columns, types):
    halves = len(p)
    samples = halves * p[0].shape[1]
    step = 512
    rows = types * mine.shape[0]
    vmem = pl.BlockSpec(memory_space=pltpu.VMEM)
    return pl.pallas_call(
        functools.partial(own_kernel, types, step, halves),
        in_specs=[vmem] * (2 * halves + 1),
        out_specs=[vmem] * 2,
        out_shape=[
            jax.ShapeDtypeStruct((rows, columns), F32),
            jax.ShapeDtypeStruct((types, samples), F32),
        ],
        scratch_shapes=[pltpu.VMEM((rows, step), BF16)],
        compiler_params=pltpu.CompilerParams(vmem_limit_bytes=VMEM_LIMIT),
        cost_estimate=pl.CostEstimate(
            flops=2 * rows * samples * columns, bytes_accessed=2 * samples * columns, transcendentals=0
        ),
        name="own_products",
    )(*p, *held, mine)


def finish_kernel(types, step, scale, own, halves, peers, *refs):
    p_in, held, mine = refs[:halves], refs[halves : 2 * halves], refs[2 * halves]
    before = refs[2 * halves + 1]
    refs = refs[2 * halves + 2 :]
    smalls, corrs, blocks = refs[: 1 + peers], refs[1 + peers : 2 + 2 * peers], refs[2 + 2 * peers : 2 + 3 * peers]
    out, left, turned, last, ready, sems = refs[2 + 3 * peers :]
    n_mine = mine.shape[0]
    genes, columns = held[0].shape[1], before.shape[1]

    small = smalls[0][...]
    corr = corrs[0][...]
    for i in range(peers):
        small = small + smalls[1 + i][...]
        corr = corr + corrs[1 + i][...]
    corr = corr[:, 0:64] + (corr[:, 64:128] + corr[:, 128:192])
    corr_t = corr.T
    low, inv = cholesky(entries(small[ROWS:, :LANES]), types)
    like = (1, genes)
    low = {key: wide(value, like) for key, value in low.items()}
    inv = [wide(value, like) for value in inv]
    coef = substitute(low, inv, [small[k : k + 1] for k in range(types)])
    coef = jnp.concatenate(coef + [jnp.zeros((ROWS - types, genes), F32)], axis=0)
    q = split3(coef)
    right = stacked([q[0], q[1], q[2], q[0], q[1], q[0]], 48)
    for k in range(types):
        c = split3(corr_t[ROWS * k : ROWS * (k + 1)])
        turned[:, k * n_mine : (k + 1) * n_mine] = jnp.concatenate(
            [c[0], c[0], c[0], c[1], c[1], c[2]], axis=0
        )
    turned_b = turned[...].astype(BF16)
    copies = []

    def write(source, begin, end):
        fitted = lax.dot_general(
            turned_b, right[:, begin:end], (((0,), (0,)), ((), ())), preferred_element_type=F32
        )
        for t in range(begin // LANES, end // LANES):
            lanes = slice(t * LANES, (t + 1) * LANES)
            here = slice(t * LANES - begin, (t + 1) * LANES - begin)
            for k in range(types):
                rows = slice(k * n_mine, k * n_mine + own)
                value = source[rows, here] - fitted[rows, here]
                for block in blocks:
                    value = value + block[k * own : (k + 1) * own, lanes]
                ready[t, pl.ds(k, own, stride=types), :] = value * scale
            copy = pltpu.make_async_copy(ready.at[t], out.at[:, pl.ds(t * LANES, LANES)], sems.at[t])
            copy.start()
            copies.append(copy)

    write(before, 0, columns)

    def add(out, first):
        if first:
            last[...] = out
        else:
            last[...] += out

    own_dot(types, step, p_in, mine, held, slice(columns, genes), left, add)
    write(last, columns, genes)
    for copy in copies:
        copy.wait()


def finish(p, mine, held, before, smalls, corrs, blocks, own, types, scale):
    halves = len(p)
    genes, columns = held[0].shape[1], before.shape[1]
    step = 512
    rows = types * mine.shape[0]
    vmem = pl.BlockSpec(memory_space=pltpu.VMEM)
    return pl.pallas_call(
        functools.partial(finish_kernel, types, step, scale, own, halves, len(blocks)),
        in_specs=[vmem] * (2 * halves + 2 + 2 * len(smalls) + len(blocks)),
        out_specs=pl.BlockSpec(memory_space=pl.ANY),
        out_shape=jax.ShapeDtypeStruct((types * own, genes), F32),
        scratch_shapes=[
            pltpu.VMEM((rows, step), BF16),
            pltpu.VMEM((48, rows), F32),
            pltpu.VMEM((rows, genes - columns), F32),
            pltpu.VMEM((genes // LANES, types * own, LANES), F32),
            pltpu.SemaphoreType.DMA((genes // LANES,)),
        ],
        compiler_params=pltpu.CompilerParams(vmem_limit_bytes=VMEM_LIMIT),
        name="finish",
    )(*p, *held, mine, before, *smalls, *corrs, *blocks)


def exchange_all(part, n_gene):
    def swap(offset):
        return lax.ppermute(part, "gene", [(i, i ^ offset) for i in range(n_gene)])

    return (part, swap(2), swap(3), swap(1))


def local(n_gene, n_sample, n_variant, expression, profile, dosage, signature):
    s_dev, g_dev = expression.shape
    v_dev = dosage.shape[1]
    types = profile.shape[1]
    own = v_dev // n_sample
    scale = 1.0 / math.sqrt(s_dev * n_sample)
    halves = 2 if n_variant % 2 == 0 else 1
    half = s_dev // halves

    held, part = right_sides(expression, profile.T, signature, halves)
    parts = exchange_all(part, n_gene)
    mine, others, *far = prepare(dosage, expression, own, halves)
    held = [held] + far
    solved = [solve(parts, types)]
    if halves == 2:
        pairs = [(i, i ^ 1) for i in range(n_variant)]
        solved.append(lax.ppermute(solved[0], "variant", pairs))
    sums = None
    for i in range(halves):
        sums = others_products(solved[i], mine, others, held[i], i * half, sums, types)
    cross_oth, small, corr_own, corr_oth = sums
    n_mine, n_oth = mine.shape[0], others.shape[0]
    blocks, smalls, corrs = [], [small], [corr_own]
    for d in range(1, n_sample):
        pairs = [(i, (i + d) % n_sample) for i in range(n_sample)]
        cross, corr = cross_oth, corr_oth
        if n_oth != own:
            cut = slice((d - 1) * own, d * own)
            cross = cross.reshape(types, n_oth, g_dev)[:, cut].reshape(types * own, g_dev)
            corr = jnp.pad(corr[cut], ((0, n_mine - own), (0, 0)))
        smalls.append(lax.ppermute(small, "sample", pairs))
        corrs.append(lax.ppermute(corr, "sample", pairs))
        blocks.append(lax.ppermute(cross, "sample", pairs))
    columns = g_dev * 3 // 4 // LANES * LANES
    before, props_t = own_products(solved, mine, held, columns, types)
    interaction = finish(
        solved, mine, held, before, smalls, corrs, blocks, own, types, scale
    )
    return interaction, props_t.T


def solution(mesh):
    placed = (P("sample", "gene"), P("gene", None), P("sample", "variant"), P())
    sizes = [mesh.shape[axis] for axis in ("gene", "sample", "variant")]
    return jax.shard_map(
        functools.partial(local, *sizes),
        mesh=mesh,
        in_specs=placed,
        out_specs=(P(("variant", "sample"), "gene"), P("sample", None)),
        check_vma=False,
    )
```

```python
import functools
import math

import jax
import jax.numpy as jnp
from jax import lax
from jax.experimental import pallas as pl
from jax.experimental.pallas import tpu as pltpu
from jax.sharding import PartitionSpec as P

F32 = jnp.float32
BF16 = jnp.bfloat16
VMEM_LIMIT = 32 << 20
LANES = 128
ROWS = 8
RHS_PIECES = 2


def round_up(n, m):
    return (n + m - 1) // m * m


def in_hbm(x):
    return pltpu.with_memory_space_constraint(x, pltpu.HBM)


def split3(x):
    hi = x.astype(BF16).astype(F32)
    rest = x - hi
    mid = rest.astype(BF16).astype(F32)
    return hi, mid, rest - mid


def stacked(parts, rows):
    have = sum(p.shape[0] for p in parts)
    if have < rows:
        parts = list(parts) + [jnp.zeros((rows - have, parts[0].shape[1]), F32)]
    return jnp.concatenate(parts, axis=0).astype(BF16)


def cholesky(entry, n):
    low = {}
    inv = []
    for j in range(n):
        d = entry(j, j)
        for k in range(j):
            d = d - low[j, k] * low[j, k]
        root = lax.rsqrt(d)
        root = root * (1.5 - 0.5 * d * root * root)
        inv.append(root)
        for i in range(j + 1, n):
            v = entry(i, j)
            for k in range(j):
                v = v - low[i, k] * low[j, k]
            low[i, j] = v * root
    return low, inv


def substitute(low, inv, right):
    n = len(right)
    y = []
    for i in range(n):
        v = right[i]
        for k in range(i):
            v = v - low[i, k] * y[k]
        y.append(v * inv[i])
    x = [None] * n
    for i in reversed(range(n)):
        v = y[i]
        for k in range(i + 1, n):
            v = v - low[k, i] * x[k]
        x[i] = v * inv[i]
    return x


def entries(tile):
    cache = {}

    def entry(i, j):
        if (i, j) not in cache:
            cache[i, j] = jnp.broadcast_to(tile[i : i + 1, j : j + 1], (ROWS, LANES))
        return cache[i, j]

    return entry


def inner_products(x, n):
    col = lax.broadcasted_iota(jnp.int32, (ROWS, LANES), 1)
    out = jnp.zeros((ROWS, LANES), F32)
    for j in range(n):
        out = jnp.where(col == j, jnp.sum(x * x[j : j + 1], axis=1, keepdims=True), out)
    return out


def wide(tile, like):
    rows, cols = like
    if rows == 1:
        return jnp.concatenate([tile[0:1]] * (cols // LANES), axis=1)
    return jnp.concatenate([tile] * (rows // ROWS), axis=0)


def rhs_kernel(
    types, halves, pieces, signature_in, profile_in, expression, held, parts, signature, profile, sems, few
):
    samples, genes = held.shape
    step = samples // pieces
    early = [
        pltpu.make_async_copy(signature_in, signature, few.at[0]),
        pltpu.make_async_copy(profile_in, profile, few.at[1]),
    ]
    for copy in early:
        copy.start()
    start = lax.rem(lax.axis_index("variant"), halves) * samples
    copies = []
    for i in range(pieces):
        rows = pl.ds(i * step, step)
        there = pl.ds(pl.multiple_of(start + i * step, step), step)
        copy = pltpu.make_async_copy(expression.at[there], held.at[rows], sems.at[i])
        copy.start()
        copies.append(copy)

    for copy in early:
        copy.wait()
    groups = genes // LANES
    base = lax.axis_index("gene") * genes
    shape = (groups, LANES)
    ids = (
        base
        + lax.broadcasted_iota(jnp.int32, shape, 0) * LANES
        + lax.broadcasted_iota(jnp.int32, shape, 1)
    )

    n_sig = signature.shape[0]
    unroll = 10 if n_sig % 10 == 0 else 1

    def look(i, member):
        for u in range(unroll):
            member = member | (ids == signature[i * unroll + u]).astype(jnp.int32)
        return member

    member = lax.fori_loop(0, n_sig // unroll, look, jnp.zeros(shape, jnp.int32))
    member = (member > 0).astype(F32)
    row = jnp.concatenate([member[h : h + 1] for h in range(groups)], axis=1)
    masked = profile[...] * row
    masked = jnp.concatenate([masked, jnp.zeros((ROWS - types, genes), F32)], axis=0)
    left = stacked(split3(masked), 32)
    parts[types * samples // LANES :, :] = inner_products(masked, types)

    for i in range(pieces):
        copies[i].wait()
        out = lax.dot_general(
            left,
            held[i * step : (i + 1) * step, :],
            (((1,), (1,)), ((), ())),
            preferred_element_type=F32,
        )
        out = out[0:ROWS] + (out[ROWS : 2 * ROWS] + out[2 * ROWS : 3 * ROWS])
        for c in range(step // LANES):
            at = (i * step // LANES + c) * types
            parts[at : at + types, :] = out[:types, c * LANES : (c + 1) * LANES]


def right_sides(expression, profile_t, signature, halves):
    samples, genes = expression.shape
    samples = samples // halves
    types = profile_t.shape[0]
    pieces = RHS_PIECES
    rows = types * samples // LANES + ROWS
    return pl.pallas_call(
        functools.partial(rhs_kernel, types, halves, pieces),
        in_specs=[pl.BlockSpec(memory_space=pltpu.HBM)] * 3,
        out_specs=[pl.BlockSpec(memory_space=pltpu.VMEM)] * 2,
        out_shape=[
            pltpu.VMEM((samples, genes), BF16),
            jax.ShapeDtypeStruct((rows, LANES), F32),
        ],
        scratch_shapes=[
            pltpu.SMEM(signature.shape, jnp.int32),
            pltpu.VMEM(profile_t.shape, F32),
            pltpu.SemaphoreType.DMA((pieces,)),
            pltpu.SemaphoreType.DMA((2,)),
        ],
        compiler_params=pltpu.CompilerParams(vmem_limit_bytes=VMEM_LIMIT),
        cost_estimate=pl.CostEstimate(
            flops=2 * 32 * samples * genes, bytes_accessed=2 * samples * genes, transcendentals=0
        ),
        name="right_sides",
    )(in_hbm(signature), in_hbm(profile_t), in_hbm(expression))


def prepare_kernel(own, halves, pieces, dosage_in, expression, first, rest, *refs):
    held = refs[:-3]
    dosage, sems, far_sem = refs[-3:]
    samples, variants = dosage.shape
    half = samples // halves
    step = samples // pieces
    side = lax.rem(lax.axis_index("variant"), halves)
    copies = []
    for i in range(pieces):
        near = i * step // half
        begin = lax.rem(side + near, halves) * half + (i * step - near * half)
        there = pl.ds(pl.multiple_of(begin, step), step)
        copy = pltpu.make_async_copy(dosage_in.at[there], dosage.at[pl.ds(i * step, step)], sems.at[i])
        copy.start()
        copies.append(copy)
    far = []
    for ref in held:
        there = pl.ds(pl.multiple_of((1 - side) * half, half), half)
        copy = pltpu.make_async_copy(expression.at[there], ref, far_sem)
        copy.start()
        far.append(copy)
    shift = lax.rem(variants - lax.axis_index("sample") * own, variants)
    for i in range(pieces):
        copies[i].wait()
        cols = slice(i * step, (i + 1) * step)
        turned = pltpu.roll(dosage[cols, :].astype(F32), shift, 1).T
        first[:, cols] = stacked([turned[:own]], first.shape[0])
        rest[:, cols] = stacked([turned[own:]], rest.shape[0])
    for copy in far:
        copy.wait()


def prepare(dosage, expression, own, halves):
    samples, variants = dosage.shape
    genes = expression.shape[1]
    pieces = 4
    first, rest = round_up(own, 16), round_up(variants - own, 16)
    return pl.pallas_call(
        functools.partial(prepare_kernel, own, halves, pieces),
        in_specs=[pl.BlockSpec(memory_space=pltpu.HBM)] * 2,
        out_specs=[pl.BlockSpec(memory_space=pltpu.VMEM)] * (1 + halves),
        out_shape=[pltpu.VMEM((first, samples), BF16), pltpu.VMEM((rest, samples), BF16)]
        + [pltpu.VMEM((samples // halves, genes), BF16)] * (halves - 1),
        scratch_shapes=[
            pltpu.VMEM(dosage.shape, jnp.int32),
            pltpu.SemaphoreType.DMA((pieces,)),
            pltpu.SemaphoreType.DMA,
        ],
        compiler_params=pltpu.CompilerParams(vmem_limit_bytes=VMEM_LIMIT),
        cost_estimate=pl.CostEstimate(
            flops=samples * variants, bytes_accessed=6 * samples * variants, transcendentals=0
        ),
        name="prepare",
    )(in_hbm(dosage), in_hbm(expression))


def solve_kernel(types, own_parts, x_parts, y_parts, d_parts, solved, packed):
    groups = (own_parts.shape[0] - ROWS) // types
    last = types * groups

    def total(rows):
        return (own_parts[rows, :] + x_parts[rows, :]) + (y_parts[rows, :] + d_parts[rows, :])

    low, inv = cholesky(entries(total(slice(last, last + ROWS))), types)
    like = (groups, LANES)
    low = {key: wide(value, like) for key, value in low.items()}
    inv = [wide(value, like) for value in inv]
    x = substitute(low, inv, [total(pl.ds(k, groups, stride=types)) for k in range(types)])
    for k in range(types):
        packed[pl.ds(k, groups, stride=ROWS), :] = x[k]
    for k in range(types, ROWS):
        packed[pl.ds(k, groups, stride=ROWS), :] = jnp.zeros(like, F32)
    for g in range(groups):
        solved[:, g * LANES : (g + 1) * LANES] = packed[g * ROWS : (g + 1) * ROWS, :]


def solve(parts, types):
    groups = (parts[0].shape[0] - ROWS) // types
    vmem = pl.BlockSpec(memory_space=pltpu.VMEM)
    return pl.pallas_call(
        functools.partial(solve_kernel, types),
        in_specs=[vmem] * 4,
        out_specs=vmem,
        out_shape=jax.ShapeDtypeStruct((ROWS, groups * LANES), F32),
        scratch_shapes=[pltpu.VMEM((groups * ROWS, LANES), F32)],
        compiler_params=pltpu.CompilerParams(vmem_limit_bytes=VMEM_LIMIT),
        name="solve",
    )(*parts)


def design_rows(left, dosage, rounded, cols, count):
    types = len(rounded)
    width = rounded[0].shape[1]
    for k in range(types):
        spread = jnp.broadcast_to(rounded[k], (16, width)).astype(BF16)
        for q in range(count // 16):
            at = k * count + q * 16
            left[at : at + 16, :] = dosage[q * 16 : q * 16 + 16, cols] * spread


def others_kernel(types, step, first_col, has_before, *refs):
    p_in, mine, others, held = refs[:4]
    before = refs[4:8] if has_before else None
    cross, small, corr_own, corr_oth, left, weights = refs[-6:]
    samples, genes = held.shape
    n_rows = types * others.shape[0]

    pp = inner_products(p_in[...], types)
    small[ROWS:, :] = jnp.concatenate([pp, jnp.zeros((ROWS, genes - LANES), F32)], axis=1)
    if has_before:
        small[ROWS:, :LANES] += before[1][ROWS:, :LANES]

    for c in range(samples // step):
        here = slice(c * step, (c + 1) * step)
        cols = slice(first_col + c * step, first_col + (c + 1) * step)
        p = p_in[:, here]
        pieces = split3(p)
        rounded = [pieces[0][k : k + 1] for k in range(types)]
        design_rows(left, others, rounded, cols, others.shape[0])
        left[n_rows:, :] = stacked(pieces, 32)
        w = jnp.concatenate([r * p for r in rounded], axis=0)
        high = w.astype(BF16).astype(F32)
        weights[:64, :] = stacked([high], 64)
        weights[64:, :] = stacked([w - high], 64)
        out = jnp.dot(left[...], held[here, :], preferred_element_type=F32)
        contract = (((1,), (1,)), ((), ()))
        both = jnp.concatenate([others[:, cols], mine[:, cols]], axis=0)
        both = lax.dot_general(both, weights[...], contract, preferred_element_type=F32)
        co, cm = both[: others.shape[0]], both[others.shape[0] :]
        py = out[n_rows : n_rows + ROWS] + (
            out[n_rows + ROWS : n_rows + 2 * ROWS] + out[n_rows + 2 * ROWS : n_rows + 3 * ROWS]
        )
        old = None
        if c:
            old = (cross, small, corr_own, corr_oth)
        elif has_before:
            old = before
        if old is None:
            cross[...] = out[:n_rows]
            small[:ROWS, :] = py
            corr_own[...] = cm
            corr_oth[...] = co
        else:
            cross[...] = old[0][...] + out[:n_rows]
            small[:ROWS, :] = old[1][:ROWS, :] + py
            corr_own[...] = old[2][...] + cm
            corr_oth[...] = old[3][...] + co


def others_products(p, mine, others, held, first_col, before, types):
    samples, genes = held.shape
    step = 512
    n_mine, n_others = mine.shape[0], others.shape[0]
    vmem = pl.BlockSpec(memory_space=pltpu.VMEM)
    before = list(before or [])
    return pl.pallas_call(
        functools.partial(others_kernel, types, step, first_col, bool(before)),
        in_specs=[vmem] * (4 + len(before)),
        out_specs=[vmem] * 4,
        out_shape=[
            jax.ShapeDtypeStruct((types * n_others, genes), F32),
            jax.ShapeDtypeStruct((2 * ROWS, genes), F32),
            jax.ShapeDtypeStruct((n_mine, 128), F32),
            jax.ShapeDtypeStruct((n_others, 128), F32),
        ],
        scratch_shapes=[
            pltpu.VMEM((types * n_others + 32, step), BF16),
            pltpu.VMEM((128, step), BF16),
        ],
        compiler_params=pltpu.CompilerParams(vmem_limit_bytes=VMEM_LIMIT),
        cost_estimate=pl.CostEstimate(
            flops=2 * types * n_others * samples * genes,
            bytes_accessed=2 * samples * genes,
            transcendentals=0,
        ),
        name="others_products",
    )(p, mine, others, held, *before)


def own_dot(types, step, first_col, p_ref, mine, held, lanes, left, add):
    for c in range(held.shape[0] // step):
        here = slice(c * step, (c + 1) * step)
        cols = slice(first_col + c * step, first_col + (c + 1) * step)
        rounded = p_ref[:, here].astype(BF16).astype(F32)
        design_rows(left, mine, [rounded[k : k + 1] for k in range(types)], cols, mine.shape[0])
        add(jnp.dot(left[...], held[here, lanes], preferred_element_type=F32), first_col + c == 0)


def own_kernel(types, step, halves, *refs):
    p_in, held, mine = refs[:halves], refs[halves : 2 * halves], refs[2 * halves]
    cross, left = refs[2 * halves + 1 :]
    half = p_in[0].shape[1]

    def add(out, first):
        if first:
            cross[...] = out
        else:
            cross[...] += out

    lanes = slice(0, cross.shape[1])
    for i in range(halves):
        own_dot(types, step, i * half, p_in[i], mine, held[i], lanes, left, add)


def own_products(p, mine, held, columns, types):
    halves = len(p)
    samples = halves * p[0].shape[1]
    step = 512
    rows = types * mine.shape[0]
    vmem = pl.BlockSpec(memory_space=pltpu.VMEM)
    return pl.pallas_call(
        functools.partial(own_kernel, types, step, halves),
        in_specs=[vmem] * (2 * halves + 1),
        out_specs=vmem,
        out_shape=jax.ShapeDtypeStruct((rows, columns), F32),
        scratch_shapes=[pltpu.VMEM((rows, step), BF16)],
        compiler_params=pltpu.CompilerParams(vmem_limit_bytes=VMEM_LIMIT),
        cost_estimate=pl.CostEstimate(
            flops=2 * rows * samples * columns, bytes_accessed=2 * samples * columns, transcendentals=0
        ),
        name="own_products",
    )(*p, *held, mine)


def finish_kernel(types, step, scale, own, halves, peers, *refs):
    p_in, held, mine = refs[:halves], refs[halves : 2 * halves], refs[2 * halves]
    before = refs[2 * halves + 1]
    refs = refs[2 * halves + 2 :]
    smalls, corrs, blocks = refs[: 1 + peers], refs[1 + peers : 2 + 2 * peers], refs[2 + 2 * peers : 2 + 3 * peers]
    out, props_out, left, turned, last, ready, sems, props, props_sems = refs[2 + 3 * peers :]
    n_mine = mine.shape[0]
    genes, columns = held[0].shape[1], before.shape[1]

    half = p_in[0].shape[1]
    side = lax.rem(lax.axis_index("variant"), halves)
    copies = []
    for i in range(halves):
        at = pl.multiple_of(lax.rem(side + i, halves) * half, half)
        props[i] = p_in[i][:types, :]
        copy = pltpu.make_async_copy(props.at[i], props_out.at[:, pl.ds(at, half)], props_sems.at[i])
        copy.start()
        copies.append(copy)
    lanes = slice(columns, genes)

    def add(out, first):
        if first:
            last[...] = out
        else:
            last[...] += out

    own_dot(types, step, 0, p_in[0], mine, held[0], lanes, left, add)

    small = smalls[0][...]
    corr = corrs[0][...]
    for i in range(peers):
        small = small + smalls[1 + i][...]
        corr = corr + corrs[1 + i][...]
    corr = corr[:, 0:64] + corr[:, 64:128]
    corr_t = corr.T
    low, inv = cholesky(entries(small[ROWS:, :LANES]), types)
    like = (1, genes)
    low = {key: wide(value, like) for key, value in low.items()}
    inv = [wide(value, like) for value in inv]
    coef = substitute(low, inv, [small[k : k + 1] for k in range(types)])
    coef = jnp.concatenate(coef + [jnp.zeros((ROWS - types, genes), F32)], axis=0)
    q = split3(coef)
    right = stacked([q[0], q[1], q[2], q[0], q[1], q[0]], 48)
    for k in range(types):
        c = split3(corr_t[ROWS * k : ROWS * (k + 1)])
        turned[:, k * n_mine : (k + 1) * n_mine] = jnp.concatenate(
            [c[0], c[0], c[0], c[1], c[1], c[2]], axis=0
        )
    turned_b = turned[...].astype(BF16)

    def write(source, begin, end):
        fitted = lax.dot_general(
            turned_b, right[:, begin:end], (((0,), (0,)), ((), ())), preferred_element_type=F32
        )
        for t in range(begin // LANES, end // LANES):
            tile = slice(t * LANES, (t + 1) * LANES)
            here = slice(t * LANES - begin, (t + 1) * LANES - begin)
            for k in range(types):
                rows = slice(k * n_mine, k * n_mine + own)
                value = source[rows, here] - fitted[rows, here]
                for block in blocks:
                    value = value + block[k * own : (k + 1) * own, tile]
                ready[t, pl.ds(k, own, stride=types), :] = value * scale
            copy = pltpu.make_async_copy(ready.at[t], out.at[:, pl.ds(t * LANES, LANES)], sems.at[t])
            copy.start()
            copies.append(copy)

    write(before, 0, columns)
    for i in range(1, halves):
        own_dot(types, step, i * half, p_in[i], mine, held[i], lanes, left, add)
    write(last, columns, genes)
    for copy in copies:
        copy.wait()


def finish(p, mine, held, before, smalls, corrs, blocks, own, types, scale):
    halves = len(p)
    genes, columns = held[0].shape[1], before.shape[1]
    step = 512
    rows = types * mine.shape[0]
    vmem = pl.BlockSpec(memory_space=pltpu.VMEM)
    return pl.pallas_call(
        functools.partial(finish_kernel, types, step, scale, own, halves, len(blocks)),
        in_specs=[vmem] * (2 * halves + 2 + 2 * len(smalls) + len(blocks)),
        out_specs=[pl.BlockSpec(memory_space=pl.ANY)] * 2,
        out_shape=[
            jax.ShapeDtypeStruct((types * own, genes), F32),
            jax.ShapeDtypeStruct((types, halves * p[0].shape[1]), F32),
        ],
        scratch_shapes=[
            pltpu.VMEM((rows, step), BF16),
            pltpu.VMEM((48, rows), F32),
            pltpu.VMEM((rows, genes - columns), F32),
            pltpu.VMEM((genes // LANES, types * own, LANES), F32),
            pltpu.SemaphoreType.DMA((genes // LANES,)),
            pltpu.VMEM((halves, types, p[0].shape[1]), F32),
            pltpu.SemaphoreType.DMA((halves,)),
        ],
        compiler_params=pltpu.CompilerParams(vmem_limit_bytes=VMEM_LIMIT),
        name="finish",
    )(*p, *held, mine, before, *smalls, *corrs, *blocks)


def exchange_all(part, n_gene):
    def swap(offset):
        return lax.ppermute(part, "gene", [(i, i ^ offset) for i in range(n_gene)])

    return (part, swap(2), swap(3), swap(1))


def local(n_gene, n_sample, n_variant, expression, profile, dosage, signature):
    s_dev, g_dev = expression.shape
    v_dev = dosage.shape[1]
    types = profile.shape[1]
    own = v_dev // n_sample
    scale = 1.0 / math.sqrt(s_dev * n_sample)
    halves = 2 if n_variant % 2 == 0 else 1
    half = s_dev // halves

    held, part = right_sides(expression, profile.T, signature, halves)
    parts = exchange_all(part, n_gene)
    mine, others, *far = prepare(dosage, expression, own, halves)
    held = [held] + far
    solved = [solve(parts, types)]
    if halves == 2:
        pairs = [(i, i ^ 1) for i in range(n_variant)]
        solved.append(lax.ppermute(solved[0], "variant", pairs))
    sums = None
    for i in range(halves):
        sums = others_products(solved[i], mine, others, held[i], i * half, sums, types)
    cross_oth, small, corr_own, corr_oth = sums
    n_mine, n_oth = mine.shape[0], others.shape[0]
    blocks, smalls, corrs = [], [small], [corr_own]
    for d in range(1, n_sample):
        pairs = [(i, (i + d) % n_sample) for i in range(n_sample)]
        cross, corr = cross_oth, corr_oth
        if n_oth != own:
            cut = slice((d - 1) * own, d * own)
            cross = cross.reshape(types, n_oth, g_dev)[:, cut].reshape(types * own, g_dev)
            corr = jnp.pad(corr[cut], ((0, n_mine - own), (0, 0)))
        smalls.append(lax.ppermute(small, "sample", pairs))
        corrs.append(lax.ppermute(corr, "sample", pairs))
        blocks.append(lax.ppermute(cross, "sample", pairs))
    columns = g_dev * 3 // 4 // LANES * LANES
    before = own_products(solved, mine, held, columns, types)
    interaction, props_t = finish(
        solved, mine, held, before, smalls, corrs, blocks, own, types, scale
    )
    return interaction, props_t.T


def solution(mesh):
    placed = (P("sample", "gene"), P("gene", None), P("sample", "variant"), P())
    sizes = [mesh.shape[axis] for axis in ("gene", "sample", "variant")]
    return jax.shard_map(
        functools.partial(local, *sizes),
        mesh=mesh,
        in_specs=placed,
        out_specs=(P(("variant", "sample"), "gene"), P("sample", None)),
        check_vma=False,
    )
```

```python
import functools
import math

import jax
import jax.numpy as jnp
from jax import lax
from jax.experimental import pallas as pl
from jax.experimental.pallas import tpu as pltpu
from jax.sharding import PartitionSpec as P

F32 = jnp.float32
BF16 = jnp.bfloat16
VMEM_LIMIT = 32 << 20
LANES = 128
ROWS = 8
RHS_PIECES = 2


def round_up(n, m):
    return (n + m - 1) // m * m


def in_hbm(x):
    return pltpu.with_memory_space_constraint(x, pltpu.HBM)


def split3(x):
    hi = x.astype(BF16).astype(F32)
    rest = x - hi
    mid = rest.astype(BF16).astype(F32)
    return hi, mid, rest - mid


def stacked(parts, rows):
    have = sum(p.shape[0] for p in parts)
    if have < rows:
        parts = list(parts) + [jnp.zeros((rows - have, parts[0].shape[1]), F32)]
    return jnp.concatenate(parts, axis=0).astype(BF16)


def cholesky(entry, n):
    low = {}
    inv = []
    for j in range(n):
        d = entry(j, j)
        for k in range(j):
            d = d - low[j, k] * low[j, k]
        root = lax.rsqrt(d)
        root = root * (1.5 - 0.5 * d * root * root)
        inv.append(root)
        for i in range(j + 1, n):
            v = entry(i, j)
            for k in range(j):
                v = v - low[i, k] * low[j, k]
            low[i, j] = v * root
    return low, inv


def substitute(low, inv, right):
    n = len(right)
    y = []
    for i in range(n):
        v = right[i]
        for k in range(i):
            v = v - low[i, k] * y[k]
        y.append(v * inv[i])
    x = [None] * n
    for i in reversed(range(n)):
        v = y[i]
        for k in range(i + 1, n):
            v = v - low[k, i] * x[k]
        x[i] = v * inv[i]
    return x


def entries(tile):
    cache = {}

    def entry(i, j):
        if (i, j) not in cache:
            cache[i, j] = jnp.broadcast_to(tile[i : i + 1, j : j + 1], (ROWS, LANES))
        return cache[i, j]

    return entry


def inner_products(x, n):
    col = lax.broadcasted_iota(jnp.int32, (ROWS, LANES), 1)
    out = jnp.zeros((ROWS, LANES), F32)
    for j in range(n):
        out = jnp.where(col == j, jnp.sum(x * x[j : j + 1], axis=1, keepdims=True), out)
    return out


def wide(tile, like):
    rows, cols = like
    if rows == 1:
        return jnp.concatenate([tile[0:1]] * (cols // LANES), axis=1)
    return jnp.concatenate([tile] * (rows // ROWS), axis=0)


def rhs_kernel(
    types, halves, pieces, signature_in, profile_in, expression, held, parts, signature, profile, sems, few
):
    samples, genes = held.shape
    step = samples // pieces
    early = [
        pltpu.make_async_copy(signature_in, signature, few.at[0]),
        pltpu.make_async_copy(profile_in, profile, few.at[1]),
    ]
    for copy in early:
        copy.start()
    start = lax.rem(lax.axis_index("variant"), halves) * samples
    copies = []
    for i in range(pieces):
        rows = pl.ds(i * step, step)
        there = pl.ds(pl.multiple_of(start + i * step, step), step)
        copy = pltpu.make_async_copy(expression.at[there], held.at[rows], sems.at[i])
        copy.start()
        copies.append(copy)

    for copy in early:
        copy.wait()
    groups = genes // LANES
    base = lax.axis_index("gene") * genes
    shape = (groups, LANES)
    ids = (
        base
        + lax.broadcasted_iota(jnp.int32, shape, 0) * LANES
        + lax.broadcasted_iota(jnp.int32, shape, 1)
    )

    n_sig = signature.shape[0]
    unroll = 10 if n_sig % 10 == 0 else 1

    def look(i, member):
        for u in range(unroll):
            member = member | (ids == signature[i * unroll + u]).astype(jnp.int32)
        return member

    member = lax.fori_loop(0, n_sig // unroll, look, jnp.zeros(shape, jnp.int32))
    member = (member > 0).astype(F32)
    row = jnp.concatenate([member[h : h + 1] for h in range(groups)], axis=1)
    masked = profile[...] * row
    masked = jnp.concatenate([masked, jnp.zeros((ROWS - types, genes), F32)], axis=0)
    left = stacked(split3(masked), 32)
    parts[types * samples // LANES :, :] = inner_products(masked, types)

    for i in range(pieces):
        copies[i].wait()
        out = lax.dot_general(
            left,
            held[i * step : (i + 1) * step, :],
            (((1,), (1,)), ((), ())),
            preferred_element_type=F32,
        )
        out = out[0:ROWS] + (out[ROWS : 2 * ROWS] + out[2 * ROWS : 3 * ROWS])
        for c in range(step // LANES):
            at = (i * step // LANES + c) * types
            parts[at : at + types, :] = out[:types, c * LANES : (c + 1) * LANES]


def right_sides(expression, profile_t, signature, halves):
    samples, genes = expression.shape
    samples = samples // halves
    types = profile_t.shape[0]
    pieces = RHS_PIECES
    rows = types * samples // LANES + ROWS
    return pl.pallas_call(
        functools.partial(rhs_kernel, types, halves, pieces),
        in_specs=[pl.BlockSpec(memory_space=pltpu.HBM)] * 3,
        out_specs=[pl.BlockSpec(memory_space=pltpu.VMEM)] * 2,
        out_shape=[
            pltpu.VMEM((samples, genes), BF16),
            jax.ShapeDtypeStruct((rows, LANES), F32),
        ],
        scratch_shapes=[
            pltpu.SMEM(signature.shape, jnp.int32),
            pltpu.VMEM(profile_t.shape, F32),
            pltpu.SemaphoreType.DMA((pieces,)),
            pltpu.SemaphoreType.DMA((2,)),
        ],
        compiler_params=pltpu.CompilerParams(vmem_limit_bytes=VMEM_LIMIT),
        cost_estimate=pl.CostEstimate(
            flops=2 * 32 * samples * genes, bytes_accessed=2 * samples * genes, transcendentals=0
        ),
        name="right_sides",
    )(in_hbm(signature), in_hbm(profile_t), in_hbm(expression))


def prepare_kernel(own, halves, pieces, dosage_in, expression, first, rest, *refs):
    held = refs[:-3]
    dosage, sems, far_sem = refs[-3:]
    samples, variants = dosage.shape
    half = samples // halves
    step = samples // pieces
    side = lax.rem(lax.axis_index("variant"), halves)
    copies = []
    for i in range(pieces):
        near = i * step // half
        begin = lax.rem(side + near, halves) * half + (i * step - near * half)
        there = pl.ds(pl.multiple_of(begin, step), step)
        copy = pltpu.make_async_copy(dosage_in.at[there], dosage.at[pl.ds(i * step, step)], sems.at[i])
        copy.start()
        copies.append(copy)
    far = []
    for ref in held:
        there = pl.ds(pl.multiple_of((1 - side) * half, half), half)
        copy = pltpu.make_async_copy(expression.at[there], ref, far_sem)
        copy.start()
        far.append(copy)
    shift = lax.rem(variants - lax.axis_index("sample") * own, variants)
    for i in range(pieces):
        copies[i].wait()
        cols = slice(i * step, (i + 1) * step)
        turned = pltpu.roll(dosage[cols, :].astype(F32), shift, 1).T
        first[:, cols] = stacked([turned[:own]], first.shape[0])
        rest[:, cols] = stacked([turned[own:]], rest.shape[0])
    for copy in far:
        copy.wait()


def prepare(dosage, expression, own, halves):
    samples, variants = dosage.shape
    genes = expression.shape[1]
    pieces = 4
    first, rest = round_up(own, 16), round_up(variants - own, 16)
    return pl.pallas_call(
        functools.partial(prepare_kernel, own, halves, pieces),
        in_specs=[pl.BlockSpec(memory_space=pltpu.HBM)] * 2,
        out_specs=[pl.BlockSpec(memory_space=pltpu.VMEM)] * (1 + halves),
        out_shape=[pltpu.VMEM((first, samples), BF16), pltpu.VMEM((rest, samples), BF16)]
        + [pltpu.VMEM((samples // halves, genes), BF16)] * (halves - 1),
        scratch_shapes=[
            pltpu.VMEM(dosage.shape, jnp.int32),
            pltpu.SemaphoreType.DMA((pieces,)),
            pltpu.SemaphoreType.DMA,
        ],
        compiler_params=pltpu.CompilerParams(vmem_limit_bytes=VMEM_LIMIT),
        cost_estimate=pl.CostEstimate(
            flops=samples * variants, bytes_accessed=6 * samples * variants, transcendentals=0
        ),
        name="prepare",
    )(in_hbm(dosage), in_hbm(expression))


def solve_kernel(types, own_parts, x_parts, y_parts, d_parts, solved, packed):
    groups = (own_parts.shape[0] - ROWS) // types
    last = types * groups

    def total(rows):
        return (own_parts[rows, :] + x_parts[rows, :]) + (y_parts[rows, :] + d_parts[rows, :])

    low, inv = cholesky(entries(total(slice(last, last + ROWS))), types)
    like = (groups, LANES)
    low = {key: wide(value, like) for key, value in low.items()}
    inv = [wide(value, like) for value in inv]
    x = substitute(low, inv, [total(pl.ds(k, groups, stride=types)) for k in range(types)])
    for k in range(types):
        packed[pl.ds(k, groups, stride=ROWS), :] = x[k]
    for k in range(types, ROWS):
        packed[pl.ds(k, groups, stride=ROWS), :] = jnp.zeros(like, F32)
    for g in range(groups):
        solved[:, g * LANES : (g + 1) * LANES] = packed[g * ROWS : (g + 1) * ROWS, :]


def solve(parts, types):
    groups = (parts[0].shape[0] - ROWS) // types
    vmem = pl.BlockSpec(memory_space=pltpu.VMEM)
    return pl.pallas_call(
        functools.partial(solve_kernel, types),
        in_specs=[vmem] * 4,
        out_specs=vmem,
        out_shape=jax.ShapeDtypeStruct((ROWS, groups * LANES), F32),
        scratch_shapes=[pltpu.VMEM((groups * ROWS, LANES), F32)],
        compiler_params=pltpu.CompilerParams(vmem_limit_bytes=VMEM_LIMIT),
        name="solve",
    )(*parts)


def design_rows(left, dosage, rounded, cols, count):
    types = len(rounded)
    width = rounded[0].shape[1]
    for k in range(types):
        spread = jnp.broadcast_to(rounded[k], (16, width)).astype(BF16)
        for q in range(count // 16):
            at = k * count + q * 16
            left[at : at + 16, :] = dosage[q * 16 : q * 16 + 16, cols] * spread


def others_kernel(types, step, first_col, has_before, *refs):
    p_in, mine, others, held = refs[:4]
    before = refs[4:8] if has_before else None
    cross, small, corr_own, corr_oth, left, weights = refs[-6:]
    samples, genes = held.shape
    n_rows = types * others.shape[0]

    pp = inner_products(p_in[...], types)
    small[ROWS:, :] = jnp.concatenate([pp, jnp.zeros((ROWS, genes - LANES), F32)], axis=1)
    if has_before:
        small[ROWS:, :LANES] += before[1][ROWS:, :LANES]

    for c in range(samples // step):
        here = slice(c * step, (c + 1) * step)
        cols = slice(first_col + c * step, first_col + (c + 1) * step)
        p = p_in[:, here]
        pieces = split3(p)
        rounded = [pieces[0][k : k + 1] for k in range(types)]
        design_rows(left, others, rounded, cols, others.shape[0])
        left[n_rows:, :] = stacked(pieces, 32)
        w = jnp.concatenate([r * p for r in rounded], axis=0)
        high = w.astype(BF16).astype(F32)
        weights[:64, :] = stacked([high], 64)
        weights[64:, :] = stacked([w - high], 64)
        out = jnp.dot(left[...], held[here, :], preferred_element_type=F32)
        contract = (((1,), (1,)), ((), ()))
        both = jnp.concatenate([others[:, cols], mine[:, cols]], axis=0)
        both = lax.dot_general(both, weights[...], contract, preferred_element_type=F32)
        co, cm = both[: others.shape[0]], both[others.shape[0] :]
        py = out[n_rows : n_rows + ROWS] + (
            out[n_rows + ROWS : n_rows + 2 * ROWS] + out[n_rows + 2 * ROWS : n_rows + 3 * ROWS]
        )
        old = None
        if c:
            old = (cross, small, corr_own, corr_oth)
        elif has_before:
            old = before
        if old is None:
            cross[...] = out[:n_rows]
            small[:ROWS, :] = py
            corr_own[...] = cm
            corr_oth[...] = co
        else:
            cross[...] = old[0][...] + out[:n_rows]
            small[:ROWS, :] = old[1][:ROWS, :] + py
            corr_own[...] = old[2][...] + cm
            corr_oth[...] = old[3][...] + co


def others_products(p, mine, others, held, first_col, before, types):
    samples, genes = held.shape
    step = 512
    n_mine, n_others = mine.shape[0], others.shape[0]
    vmem = pl.BlockSpec(memory_space=pltpu.VMEM)
    before = list(before or [])
    return pl.pallas_call(
        functools.partial(others_kernel, types, step, first_col, bool(before)),
        in_specs=[vmem] * (4 + len(before)),
        out_specs=[vmem] * 4,
        out_shape=[
            jax.ShapeDtypeStruct((types * n_others, genes), F32),
            jax.ShapeDtypeStruct((2 * ROWS, genes), F32),
            jax.ShapeDtypeStruct((n_mine, 128), F32),
            jax.ShapeDtypeStruct((n_others, 128), F32),
        ],
        scratch_shapes=[
            pltpu.VMEM((types * n_others + 32, step), BF16),
            pltpu.VMEM((128, step), BF16),
        ],
        compiler_params=pltpu.CompilerParams(vmem_limit_bytes=VMEM_LIMIT),
        cost_estimate=pl.CostEstimate(
            flops=2 * types * n_others * samples * genes,
            bytes_accessed=2 * samples * genes,
            transcendentals=0,
        ),
        name="others_products",
    )(p, mine, others, held, *before)


def own_dot(types, step, first_col, p_ref, mine, held, lanes, left, add, beside=None):
    count = held.shape[0] // step
    for c in range(count):
        here = slice(c * step, (c + 1) * step)
        cols = slice(first_col + c * step, first_col + (c + 1) * step)
        rounded = p_ref[:, here].astype(BF16).astype(F32)
        design_rows(left, mine, [rounded[k : k + 1] for k in range(types)], cols, mine.shape[0])
        if beside is not None:
            beside(c, count)
        add(jnp.dot(left[...], held[here, lanes], preferred_element_type=F32), first_col + c == 0)


def own_kernel(types, step, halves, *refs):
    p_in, held, mine = refs[:halves], refs[halves : 2 * halves], refs[2 * halves]
    cross, tail, left = refs[2 * halves + 1 :]
    half = p_in[0].shape[1]

    def add_to(total):
        def add(out, first):
            if first:
                total[...] = out
            else:
                total[...] += out

        return add

    columns, genes = cross.shape[1], held[0].shape[1]
    for i in range(halves):
        own_dot(types, step, i * half, p_in[i], mine, held[i], slice(0, columns), left, add_to(cross))
    own_dot(types, step, 0, p_in[0], mine, held[0], slice(columns, genes), left, add_to(tail))


def own_products(p, mine, held, columns, types):
    halves = len(p)
    samples, genes = halves * p[0].shape[1], held[0].shape[1]
    step = 512
    rows = types * mine.shape[0]
    vmem = pl.BlockSpec(memory_space=pltpu.VMEM)
    return pl.pallas_call(
        functools.partial(own_kernel, types, step, halves),
        in_specs=[vmem] * (2 * halves + 1),
        out_specs=[vmem] * 2,
        out_shape=[
            jax.ShapeDtypeStruct((rows, columns), F32),
            jax.ShapeDtypeStruct((rows, genes - columns), F32),
        ],
        scratch_shapes=[pltpu.VMEM((rows, step), BF16)],
        compiler_params=pltpu.CompilerParams(vmem_limit_bytes=VMEM_LIMIT),
        cost_estimate=pl.CostEstimate(
            flops=2 * rows * samples * columns, bytes_accessed=2 * samples * columns, transcendentals=0
        ),
        name="own_products",
    )(*p, *held, mine)


def finish_kernel(types, step, scale, own, halves, peers, *refs):
    p_in, held, mine = refs[:halves], refs[halves : 2 * halves], refs[2 * halves]
    before, tail = refs[2 * halves + 1 : 2 * halves + 3]
    refs = refs[2 * halves + 3 :]
    smalls, corrs, blocks = refs[: 1 + peers], refs[1 + peers : 2 + 2 * peers], refs[2 + 2 * peers : 2 + 3 * peers]
    out, props_out, left, turned, last, ready, sems, props, props_sems = refs[2 + 3 * peers :]
    n_mine = mine.shape[0]
    genes, columns = held[0].shape[1], before.shape[1]

    half = p_in[0].shape[1]
    side = lax.rem(lax.axis_index("variant"), halves)
    copies = []
    for i in range(halves):
        at = pl.multiple_of(lax.rem(side + i, halves) * half, half)
        props[i] = p_in[i][:types, :]
        copy = pltpu.make_async_copy(props.at[i], props_out.at[:, pl.ds(at, half)], props_sems.at[i])
        copy.start()
        copies.append(copy)
    lanes = slice(columns, genes)

    seen = [tail]

    def add(out, first):
        last[...] = seen[-1][...] + out
        seen.append(last)

    small = smalls[0][...]
    corr = corrs[0][...]
    for i in range(peers):
        small = small + smalls[1 + i][...]
        corr = corr + corrs[1 + i][...]
    corr = corr[:, 0:64] + corr[:, 64:128]
    corr_t = corr.T
    low, inv = cholesky(entries(small[ROWS:, :LANES]), types)
    like = (1, genes)
    low = {key: wide(value, like) for key, value in low.items()}
    inv = [wide(value, like) for value in inv]
    coef = substitute(low, inv, [small[k : k + 1] for k in range(types)])
    coef = jnp.concatenate(coef + [jnp.zeros((ROWS - types, genes), F32)], axis=0)
    q = split3(coef)
    right = stacked([q[0], q[1], q[2], q[0], q[1], q[0]], 48)
    for k in range(types):
        c = split3(corr_t[ROWS * k : ROWS * (k + 1)])
        turned[:, k * n_mine : (k + 1) * n_mine] = jnp.concatenate(
            [c[0], c[0], c[0], c[1], c[1], c[2]], axis=0
        )
    turned_b = turned[...].T.astype(BF16)

    def write(t):
        tile = slice(t * LANES, (t + 1) * LANES)
        source, here = before, tile
        if t * LANES >= columns:
            source, here = seen[-1], slice(t * LANES - columns, (t + 1) * LANES - columns)
        fitted = jnp.dot(turned_b, right[:, tile], preferred_element_type=F32)
        for k in range(types):
            rows = slice(k * n_mine, k * n_mine + own)
            value = source[rows, here] - fitted[rows]
            for block in blocks:
                value = value + block[k * own : (k + 1) * own, tile]
            ready[t, pl.ds(k, own, stride=types), :] = value * scale
        copy = pltpu.make_async_copy(ready.at[t], out.at[:, pl.ds(t * LANES, LANES)], sems.at[t])
        copy.start()
        copies.append(copy)

    early, tiles = columns // LANES, genes // LANES

    def beside(c, count):
        for t in range(early * c // count, early * (c + 1) // count):
            write(t)

    for i in range(1, halves):
        own_dot(
            types, step, i * half, p_in[i], mine, held[i], lanes, left, add,
            beside if i == halves - 1 else None,
        )
    for t in range(early if halves > 1 else 0, tiles):
        write(t)
    for copy in copies:
        copy.wait()


def finish(p, mine, held, before, tail, smalls, corrs, blocks, own, types, scale):
    halves = len(p)
    genes, columns = held[0].shape[1], before.shape[1]
    step = 512
    rows = types * mine.shape[0]
    vmem = pl.BlockSpec(memory_space=pltpu.VMEM)
    return pl.pallas_call(
        functools.partial(finish_kernel, types, step, scale, own, halves, len(blocks)),
        in_specs=[vmem] * (2 * halves + 3 + 2 * len(smalls) + len(blocks)),
        out_specs=[pl.BlockSpec(memory_space=pl.ANY)] * 2,
        out_shape=[
            jax.ShapeDtypeStruct((types * own, genes), F32),
            jax.ShapeDtypeStruct((types, halves * p[0].shape[1]), F32),
        ],
        scratch_shapes=[
            pltpu.VMEM((rows, step), BF16),
            pltpu.VMEM((48, rows), F32),
            pltpu.VMEM((rows, genes - columns), F32),
            pltpu.VMEM((genes // LANES, types * own, LANES), F32),
            pltpu.SemaphoreType.DMA((genes // LANES,)),
            pltpu.VMEM((halves, types, p[0].shape[1]), F32),
            pltpu.SemaphoreType.DMA((halves,)),
        ],
        compiler_params=pltpu.CompilerParams(vmem_limit_bytes=VMEM_LIMIT),
        name="finish",
    )(*p, *held, mine, before, tail, *smalls, *corrs, *blocks)


def exchange_all(part, n_gene):
    def swap(offset):
        return lax.ppermute(part, "gene", [(i, i ^ offset) for i in range(n_gene)])

    return (part, swap(2), swap(3), swap(1))


def local(n_gene, n_sample, n_variant, expression, profile, dosage, signature):
    s_dev, g_dev = expression.shape
    v_dev = dosage.shape[1]
    types = profile.shape[1]
    own = v_dev // n_sample
    scale = 1.0 / math.sqrt(s_dev * n_sample)
    halves = 2 if n_variant % 2 == 0 else 1
    half = s_dev // halves

    held, part = right_sides(expression, profile.T, signature, halves)
    parts = exchange_all(part, n_gene)
    mine, others, *far = prepare(dosage, expression, own, halves)
    held = [held] + far
    solved = [solve(parts, types)]
    if halves == 2:
        pairs = [(i, i ^ 1) for i in range(n_variant)]
        solved.append(lax.ppermute(solved[0], "variant", pairs))
    sums = None
    for i in range(halves):
        sums = others_products(solved[i], mine, others, held[i], i * half, sums, types)
    cross_oth, small, corr_own, corr_oth = sums
    n_mine, n_oth = mine.shape[0], others.shape[0]
    blocks, smalls, corrs = [], [small], [corr_own]
    for d in range(1, n_sample):
        pairs = [(i, (i + d) % n_sample) for i in range(n_sample)]
        cross, corr = cross_oth, corr_oth
        if n_oth != own:
            cut = slice((d - 1) * own, d * own)
            cross = cross.reshape(types, n_oth, g_dev)[:, cut].reshape(types * own, g_dev)
            corr = jnp.pad(corr[cut], ((0, n_mine - own), (0, 0)))
        smalls.append(lax.ppermute(small, "sample", pairs))
        corrs.append(lax.ppermute(corr, "sample", pairs))
        blocks.append(lax.ppermute(cross, "sample", pairs))
    columns = g_dev * 3 // 4 // LANES * LANES
    before, tail = own_products(solved, mine, held, columns, types)
    interaction, props_t = finish(
        solved, mine, held, before, tail, smalls, corrs, blocks, own, types, scale
    )
    return interaction, props_t.T


def solution(mesh):
    placed = (P("sample", "gene"), P("gene", None), P("sample", "variant"), P())
    sizes = [mesh.shape[axis] for axis in ("gene", "sample", "variant")]
    return jax.shard_map(
        functools.partial(local, *sizes),
        mesh=mesh,
        in_specs=placed,
        out_specs=(P(("variant", "sample"), "gene"), P("sample", None)),
        check_vma=False,
    )
```

```python
import functools
import math

import jax
import jax.numpy as jnp
from jax import lax
from jax.experimental import pallas as pl
from jax.experimental.pallas import tpu as pltpu
from jax.sharding import PartitionSpec as P

F32 = jnp.float32
BF16 = jnp.bfloat16
VMEM_LIMIT = 32 << 20
LANES = 128
ROWS = 8
RHS_PIECES = 2


def round_up(n, m):
    return (n + m - 1) // m * m


def in_hbm(x):
    return pltpu.with_memory_space_constraint(x, pltpu.HBM)


def split3(x):
    hi = x.astype(BF16).astype(F32)
    rest = x - hi
    mid = rest.astype(BF16).astype(F32)
    return hi, mid, rest - mid


def stacked(parts, rows):
    have = sum(p.shape[0] for p in parts)
    if have < rows:
        parts = list(parts) + [jnp.zeros((rows - have, parts[0].shape[1]), F32)]
    return jnp.concatenate(parts, axis=0).astype(BF16)


def cholesky(entry, n):
    low = {}
    inv = []
    for j in range(n):
        d = entry(j, j)
        for k in range(j):
            d = d - low[j, k] * low[j, k]
        root = lax.rsqrt(d)
        root = root * (1.5 - 0.5 * d * root * root)
        inv.append(root)
        for i in range(j + 1, n):
            v = entry(i, j)
            for k in range(j):
                v = v - low[i, k] * low[j, k]
            low[i, j] = v * root
    return low, inv


def substitute(low, inv, right):
    n = len(right)
    y = []
    for i in range(n):
        v = right[i]
        for k in range(i):
            v = v - low[i, k] * y[k]
        y.append(v * inv[i])
    x = [None] * n
    for i in reversed(range(n)):
        v = y[i]
        for k in range(i + 1, n):
            v = v - low[k, i] * x[k]
        x[i] = v * inv[i]
    return x


def entries(tile):
    cache = {}

    def entry(i, j):
        if (i, j) not in cache:
            cache[i, j] = jnp.broadcast_to(tile[i : i + 1, j : j + 1], (ROWS, LANES))
        return cache[i, j]

    return entry


def inner_products(x, n):
    col = lax.broadcasted_iota(jnp.int32, (ROWS, LANES), 1)
    out = jnp.zeros((ROWS, LANES), F32)
    for j in range(n):
        out = jnp.where(col == j, jnp.sum(x * x[j : j + 1], axis=1, keepdims=True), out)
    return out


def wide(tile, like):
    rows, cols = like
    if rows == 1:
        return jnp.concatenate([tile[0:1]] * (cols // LANES), axis=1)
    return jnp.concatenate([tile] * (rows // ROWS), axis=0)


def rhs_kernel(
    types, halves, pieces, signature_in, profile_in, expression, held, parts, signature, profile, sems, few
):
    samples, genes = held.shape
    step = samples // pieces
    early = [
        pltpu.make_async_copy(signature_in, signature, few.at[0]),
        pltpu.make_async_copy(profile_in, profile, few.at[1]),
    ]
    for copy in early:
        copy.start()
    start = lax.rem(lax.axis_index("variant"), halves) * samples
    copies = []
    for i in range(pieces):
        rows = pl.ds(i * step, step)
        there = pl.ds(pl.multiple_of(start + i * step, step), step)
        copy = pltpu.make_async_copy(expression.at[there], held.at[rows], sems.at[i])
        copy.start()
        copies.append(copy)

    for copy in early:
        copy.wait()
    groups = genes // LANES
    base = lax.axis_index("gene") * genes
    shape = (groups, LANES)
    ids = (
        base
        + lax.broadcasted_iota(jnp.int32, shape, 0) * LANES
        + lax.broadcasted_iota(jnp.int32, shape, 1)
    )

    n_sig = signature.shape[0]
    unroll = 10 if n_sig % 10 == 0 else 1

    def look(i, member):
        for u in range(unroll):
            member = member | (ids == signature[i * unroll + u]).astype(jnp.int32)
        return member

    member = lax.fori_loop(0, n_sig // unroll, look, jnp.zeros(shape, jnp.int32))
    member = (member > 0).astype(F32)
    row = jnp.concatenate([member[h : h + 1] for h in range(groups)], axis=1)
    masked = profile[...] * row
    masked = jnp.concatenate([masked, jnp.zeros((ROWS - types, genes), F32)], axis=0)
    left = stacked(split3(masked), 32)
    parts[types * samples // LANES :, :] = inner_products(masked, types)

    for i in range(pieces):
        copies[i].wait()
        out = lax.dot_general(
            left,
            held[i * step : (i + 1) * step, :],
            (((1,), (1,)), ((), ())),
            preferred_element_type=F32,
        )
        out = out[0:ROWS] + (out[ROWS : 2 * ROWS] + out[2 * ROWS : 3 * ROWS])
        for c in range(step // LANES):
            at = (i * step // LANES + c) * types
            parts[at : at + types, :] = out[:types, c * LANES : (c + 1) * LANES]


def right_sides(expression, profile_t, signature, halves):
    samples, genes = expression.shape
    samples = samples // halves
    types = profile_t.shape[0]
    pieces = RHS_PIECES
    rows = types * samples // LANES + ROWS
    return pl.pallas_call(
        functools.partial(rhs_kernel, types, halves, pieces),
        in_specs=[pl.BlockSpec(memory_space=pltpu.HBM)] * 3,
        out_specs=[pl.BlockSpec(memory_space=pltpu.VMEM)] * 2,
        out_shape=[
            pltpu.VMEM((samples, genes), BF16),
            jax.ShapeDtypeStruct((rows, LANES), F32),
        ],
        scratch_shapes=[
            pltpu.SMEM(signature.shape, jnp.int32),
            pltpu.VMEM(profile_t.shape, F32),
            pltpu.SemaphoreType.DMA((pieces,)),
            pltpu.SemaphoreType.DMA((2,)),
        ],
        compiler_params=pltpu.CompilerParams(vmem_limit_bytes=VMEM_LIMIT),
        cost_estimate=pl.CostEstimate(
            flops=2 * 32 * samples * genes, bytes_accessed=2 * samples * genes, transcendentals=0
        ),
        name="right_sides",
    )(in_hbm(signature), in_hbm(profile_t), in_hbm(expression))


def prepare_kernel(own, halves, pieces, dosage_in, expression, first, rest, *refs):
    held = refs[:-3]
    dosage, sems, far_sem = refs[-3:]
    samples, variants = dosage.shape
    half = samples // halves
    step = samples // pieces
    side = lax.rem(lax.axis_index("variant"), halves)
    copies = []
    for i in range(pieces):
        near = i * step // half
        begin = lax.rem(side + near, halves) * half + (i * step - near * half)
        there = pl.ds(pl.multiple_of(begin, step), step)
        copy = pltpu.make_async_copy(dosage_in.at[there], dosage.at[pl.ds(i * step, step)], sems.at[i])
        copy.start()
        copies.append(copy)
    far = []
    for ref in held:
        there = pl.ds(pl.multiple_of((1 - side) * half, half), half)
        copy = pltpu.make_async_copy(expression.at[there], ref, far_sem)
        copy.start()
        far.append(copy)
    shift = lax.rem(variants - lax.axis_index("sample") * own, variants)
    for i in range(pieces):
        copies[i].wait()
        cols = slice(i * step, (i + 1) * step)
        turned = pltpu.roll(dosage[cols, :].astype(F32), shift, 1).T
        first[:, cols] = stacked([turned[:own]], first.shape[0])
        rest[:, cols] = stacked([turned[own:]], rest.shape[0])
    for copy in far:
        copy.wait()


def prepare(dosage, expression, own, halves):
    samples, variants = dosage.shape
    genes = expression.shape[1]
    pieces = 4
    first, rest = round_up(own, 16), round_up(variants - own, 16)
    return pl.pallas_call(
        functools.partial(prepare_kernel, own, halves, pieces),
        in_specs=[pl.BlockSpec(memory_space=pltpu.HBM)] * 2,
        out_specs=[pl.BlockSpec(memory_space=pltpu.VMEM)] * (1 + halves),
        out_shape=[pltpu.VMEM((first, samples), BF16), pltpu.VMEM((rest, samples), BF16)]
        + [pltpu.VMEM((samples // halves, genes), BF16)] * (halves - 1),
        scratch_shapes=[
            pltpu.VMEM(dosage.shape, jnp.int32),
            pltpu.SemaphoreType.DMA((pieces,)),
            pltpu.SemaphoreType.DMA,
        ],
        compiler_params=pltpu.CompilerParams(vmem_limit_bytes=VMEM_LIMIT),
        cost_estimate=pl.CostEstimate(
            flops=samples * variants, bytes_accessed=6 * samples * variants, transcendentals=0
        ),
        name="prepare",
    )(in_hbm(dosage), in_hbm(expression))


def solve_kernel(types, own_parts, x_parts, y_parts, d_parts, solved, packed):
    groups = (own_parts.shape[0] - ROWS) // types
    last = types * groups

    def total(rows):
        return (own_parts[rows, :] + x_parts[rows, :]) + (y_parts[rows, :] + d_parts[rows, :])

    low, inv = cholesky(entries(total(slice(last, last + ROWS))), types)
    like = (groups, LANES)
    low = {key: wide(value, like) for key, value in low.items()}
    inv = [wide(value, like) for value in inv]
    x = substitute(low, inv, [total(pl.ds(k, groups, stride=types)) for k in range(types)])
    for k in range(types):
        packed[pl.ds(k, groups, stride=ROWS), :] = x[k]
    for k in range(types, ROWS):
        packed[pl.ds(k, groups, stride=ROWS), :] = jnp.zeros(like, F32)
    for g in range(groups):
        solved[:, g * LANES : (g + 1) * LANES] = packed[g * ROWS : (g + 1) * ROWS, :]


def solve(parts, types):
    groups = (parts[0].shape[0] - ROWS) // types
    vmem = pl.BlockSpec(memory_space=pltpu.VMEM)
    return pl.pallas_call(
        functools.partial(solve_kernel, types),
        in_specs=[vmem] * 4,
        out_specs=vmem,
        out_shape=jax.ShapeDtypeStruct((ROWS, groups * LANES), F32),
        scratch_shapes=[pltpu.VMEM((groups * ROWS + ROWS, LANES), F32)],
        compiler_params=pltpu.CompilerParams(vmem_limit_bytes=VMEM_LIMIT),
        name="solve",
    )(*parts)


def design_rows(left, dosage, rounded, cols, count):
    types = len(rounded)
    width = rounded[0].shape[1]
    for k in range(types):
        spread = jnp.broadcast_to(rounded[k], (16, width)).astype(BF16)
        for q in range(count // 16):
            at = k * count + q * 16
            left[at : at + 16, :] = dosage[q * 16 : q * 16 + 16, cols] * spread


def others_kernel(types, step, first_col, has_before, *refs):
    p_in, mine, others, held = refs[:4]
    before = refs[4:8] if has_before else None
    cross, small, corr_own, corr_oth, left, weights = refs[-6:]
    samples, genes = held.shape
    n_rows = types * others.shape[0]

    pp = inner_products(p_in[...], types)
    small[ROWS:, :] = jnp.concatenate([pp, jnp.zeros((ROWS, genes - LANES), F32)], axis=1)
    if has_before:
        small[ROWS:, :LANES] += before[1][ROWS:, :LANES]

    for c in range(samples // step):
        here = slice(c * step, (c + 1) * step)
        cols = slice(first_col + c * step, first_col + (c + 1) * step)
        p = p_in[:, here]
        pieces = split3(p)
        rounded = [pieces[0][k : k + 1] for k in range(types)]
        design_rows(left, others, rounded, cols, others.shape[0])
        left[n_rows:, :] = stacked(pieces, 32)
        w = jnp.concatenate([r * p for r in rounded], axis=0)
        high = w.astype(BF16).astype(F32)
        weights[:64, :] = stacked([high], 64)
        weights[64:, :] = stacked([w - high], 64)
        out = jnp.dot(left[...], held[here, :], preferred_element_type=F32)
        contract = (((1,), (1,)), ((), ()))
        both = jnp.concatenate([others[:, cols], mine[:, cols]], axis=0)
        both = lax.dot_general(both, weights[...], contract, preferred_element_type=F32)
        co, cm = both[: others.shape[0]], both[others.shape[0] :]
        py = out[n_rows : n_rows + ROWS] + (
            out[n_rows + ROWS : n_rows + 2 * ROWS] + out[n_rows + 2 * ROWS : n_rows + 3 * ROWS]
        )
        old = None
        if c:
            old = (cross, small, corr_own, corr_oth)
        elif has_before:
            old = before
        if old is None:
            cross[...] = out[:n_rows]
            small[:ROWS, :] = py
            corr_own[...] = cm
            corr_oth[...] = co
        else:
            cross[...] = old[0][...] + out[:n_rows]
            small[:ROWS, :] = old[1][:ROWS, :] + py
            corr_own[...] = old[2][...] + cm
            corr_oth[...] = old[3][...] + co


def others_products(p, mine, others, held, first_col, before, types):
    samples, genes = held.shape
    step = 512
    n_mine, n_others = mine.shape[0], others.shape[0]
    vmem = pl.BlockSpec(memory_space=pltpu.VMEM)
    before = list(before or [])
    return pl.pallas_call(
        functools.partial(others_kernel, types, step, first_col, bool(before)),
        in_specs=[vmem] * (4 + len(before)),
        out_specs=[vmem] * 4,
        out_shape=[
            jax.ShapeDtypeStruct((types * n_others, genes), F32),
            jax.ShapeDtypeStruct((2 * ROWS, genes), F32),
            jax.ShapeDtypeStruct((n_mine, 128), F32),
            jax.ShapeDtypeStruct((n_others, 128), F32),
        ],
        scratch_shapes=[
            pltpu.VMEM((types * n_others + 32, step), BF16),
            pltpu.VMEM((128, step), BF16),
        ],
        compiler_params=pltpu.CompilerParams(vmem_limit_bytes=VMEM_LIMIT),
        cost_estimate=pl.CostEstimate(
            flops=2 * types * n_others * samples * genes,
            bytes_accessed=2 * samples * genes,
            transcendentals=0,
        ),
        name="others_products",
    )(p, mine, others, held, *before)


def own_dot(types, step, first_col, p_ref, mine, held, lanes, left, add, beside=None):
    count = held.shape[0] // step
    for c in range(count):
        here = slice(c * step, (c + 1) * step)
        cols = slice(first_col + c * step, first_col + (c + 1) * step)
        rounded = p_ref[:, here].astype(BF16).astype(F32)
        design_rows(left, mine, [rounded[k : k + 1] for k in range(types)], cols, mine.shape[0])
        if beside is not None:
            beside(c, count)
        add(jnp.dot(left[...], held[here, lanes], preferred_element_type=F32), first_col + c == 0)


def own_kernel(types, step, halves, *refs):
    p_in, held, mine = refs[:halves], refs[halves : 2 * halves], refs[2 * halves]
    cross, tail, left = refs[2 * halves + 1 :]
    half = p_in[0].shape[1]

    def add_to(total):
        def add(out, first):
            if first:
                total[...] = out
            else:
                total[...] += out

        return add

    columns, genes = cross.shape[1], held[0].shape[1]
    for i in range(halves):
        own_dot(types, step, i * half, p_in[i], mine, held[i], slice(0, columns), left, add_to(cross))
    own_dot(types, step, 0, p_in[0], mine, held[0], slice(columns, genes), left, add_to(tail))


def own_products(p, mine, held, columns, types):
    halves = len(p)
    samples, genes = halves * p[0].shape[1], held[0].shape[1]
    step = 512
    rows = types * mine.shape[0]
    vmem = pl.BlockSpec(memory_space=pltpu.VMEM)
    return pl.pallas_call(
        functools.partial(own_kernel, types, step, halves),
        in_specs=[vmem] * (2 * halves + 1),
        out_specs=[vmem] * 2,
        out_shape=[
            jax.ShapeDtypeStruct((rows, columns), F32),
            jax.ShapeDtypeStruct((rows, genes - columns), F32),
        ],
        scratch_shapes=[pltpu.VMEM((rows, step), BF16)],
        compiler_params=pltpu.CompilerParams(vmem_limit_bytes=VMEM_LIMIT),
        cost_estimate=pl.CostEstimate(
            flops=2 * rows * samples * columns, bytes_accessed=2 * samples * columns, transcendentals=0
        ),
        name="own_products",
    )(*p, *held, mine)


def finish_kernel(types, step, scale, own, halves, peers, *refs):
    p_in, held, mine = refs[:halves], refs[halves : 2 * halves], refs[2 * halves]
    before, tail = refs[2 * halves + 1 : 2 * halves + 3]
    refs = refs[2 * halves + 3 :]
    smalls, corrs, blocks = refs[: 1 + peers], refs[1 + peers : 2 + 2 * peers], refs[2 + 2 * peers : 2 + 3 * peers]
    out, props_out, left, turned, last, ready, sems, props, props_sems = refs[2 + 3 * peers :]
    n_mine = mine.shape[0]
    genes, columns = held[0].shape[1], before.shape[1]

    half = p_in[0].shape[1]
    side = lax.rem(lax.axis_index("variant"), halves)
    copies = []
    for i in range(halves):
        at = pl.multiple_of(lax.rem(side + i, halves) * half, half)
        props[i] = p_in[i][:types, :]
        copy = pltpu.make_async_copy(props.at[i], props_out.at[:, pl.ds(at, half)], props_sems.at[i])
        copy.start()
        copies.append(copy)
    lanes = slice(columns, genes)

    seen = [tail]

    def add(out, first):
        last[...] = seen[-1][...] + out
        seen.append(last)

    small = smalls[0][...]
    corr = corrs[0][...]
    for i in range(peers):
        small = small + smalls[1 + i][...]
        corr = corr + corrs[1 + i][...]
    corr = corr[:, 0:64] + corr[:, 64:128]
    corr_t = corr.T
    low, inv = cholesky(entries(small[ROWS:, :LANES]), types)
    like = (1, genes)
    low = {key: wide(value, like) for key, value in low.items()}
    inv = [wide(value, like) for value in inv]
    coef = substitute(low, inv, [small[k : k + 1] for k in range(types)])
    coef = jnp.concatenate(coef + [jnp.zeros((ROWS - types, genes), F32)], axis=0)
    q = split3(coef)
    right = stacked([q[0], q[1], q[2], q[0], q[1], q[0]], 48)
    for k in range(types):
        c = split3(corr_t[ROWS * k : ROWS * (k + 1)])
        turned[:, k * n_mine : (k + 1) * n_mine] = jnp.concatenate(
            [c[0], c[0], c[0], c[1], c[1], c[2]], axis=0
        )
    turned_b = turned[...].T.astype(BF16)

    def write(t):
        tile = slice(t * LANES, (t + 1) * LANES)
        source, here = before, tile
        if t * LANES >= columns:
            source, here = seen[-1], slice(t * LANES - columns, (t + 1) * LANES - columns)
        fitted = jnp.dot(turned_b, right[:, tile], preferred_element_type=F32)
        for k in range(types):
            rows = slice(k * n_mine, k * n_mine + own)
            value = source[rows, here] - fitted[rows]
            for block in blocks:
                value = value + block[k * own : (k + 1) * own, tile]
            ready[t, pl.ds(k, own, stride=types), :] = value * scale
        copy = pltpu.make_async_copy(
            ready.at[t, pl.ds(0, types * own)], out.at[:, pl.ds(t * LANES, LANES)], sems.at[t]
        )
        copy.start()
        copies.append(copy)

    early, tiles = columns // LANES, genes // LANES

    def beside(c, count):
        for t in range(early * c // count, early * (c + 1) // count):
            write(t)

    for i in range(1, halves):
        own_dot(
            types, step, i * half, p_in[i], mine, held[i], lanes, left, add,
            beside if i == halves - 1 else None,
        )
    for t in range(early if halves > 1 else 0, tiles):
        write(t)
    for copy in copies:
        copy.wait()


def finish(p, mine, held, before, tail, smalls, corrs, blocks, own, types, scale):
    halves = len(p)
    genes, columns = held[0].shape[1], before.shape[1]
    step = 512
    rows = types * mine.shape[0]
    vmem = pl.BlockSpec(memory_space=pltpu.VMEM)
    return pl.pallas_call(
        functools.partial(finish_kernel, types, step, scale, own, halves, len(blocks)),
        in_specs=[vmem] * (2 * halves + 3 + 2 * len(smalls) + len(blocks)),
        out_specs=[pl.BlockSpec(memory_space=pl.ANY)] * 2,
        out_shape=[
            jax.ShapeDtypeStruct((types * own, genes), F32),
            jax.ShapeDtypeStruct((types, halves * p[0].shape[1]), F32),
        ],
        scratch_shapes=[
            pltpu.VMEM((rows, step), BF16),
            pltpu.VMEM((48, rows), F32),
            pltpu.VMEM((rows, genes - columns), F32),
            pltpu.VMEM((genes // LANES, types * own + ROWS, LANES), F32),
            pltpu.SemaphoreType.DMA((genes // LANES,)),
            pltpu.VMEM((halves, types, p[0].shape[1]), F32),
            pltpu.SemaphoreType.DMA((halves,)),
        ],
        compiler_params=pltpu.CompilerParams(vmem_limit_bytes=VMEM_LIMIT),
        name="finish",
    )(*p, *held, mine, before, tail, *smalls, *corrs, *blocks)


def exchange_all(part, n_gene):
    def swap(offset):
        return lax.ppermute(part, "gene", [(i, i ^ offset) for i in range(n_gene)])

    return (part, swap(2), swap(3), swap(1))


def local(n_gene, n_sample, n_variant, expression, profile, dosage, signature):
    s_dev, g_dev = expression.shape
    v_dev = dosage.shape[1]
    types = profile.shape[1]
    own = v_dev // n_sample
    scale = 1.0 / math.sqrt(s_dev * n_sample)
    halves = 2 if n_variant % 2 == 0 else 1
    half = s_dev // halves

    held, part = right_sides(expression, profile.T, signature, halves)
    parts = exchange_all(part, n_gene)
    mine, others, *far = prepare(dosage, expression, own, halves)
    held = [held] + far
    solved = [solve(parts, types)]
    if halves == 2:
        pairs = [(i, i ^ 1) for i in range(n_variant)]
        solved.append(lax.ppermute(solved[0], "variant", pairs))
    sums = None
    for i in range(halves):
        sums = others_products(solved[i], mine, others, held[i], i * half, sums, types)
    cross_oth, small, corr_own, corr_oth = sums
    n_mine, n_oth = mine.shape[0], others.shape[0]
    blocks, smalls, corrs = [], [small], [corr_own]
    for d in range(1, n_sample):
        pairs = [(i, (i + d) % n_sample) for i in range(n_sample)]
        cross, corr = cross_oth, corr_oth
        if n_oth != own:
            cut = slice((d - 1) * own, d * own)
            cross = cross.reshape(types, n_oth, g_dev)[:, cut].reshape(types * own, g_dev)
            corr = jnp.pad(corr[cut], ((0, n_mine - own), (0, 0)))
        smalls.append(lax.ppermute(small, "sample", pairs))
        corrs.append(lax.ppermute(corr, "sample", pairs))
        blocks.append(lax.ppermute(cross, "sample", pairs))
    columns = g_dev * 3 // 4 // LANES * LANES
    before, tail = own_products(solved, mine, held, columns, types)
    interaction, props_t = finish(
        solved, mine, held, before, tail, smalls, corrs, blocks, own, types, scale
    )
    return interaction, props_t.T


def solution(mesh):
    placed = (P("sample", "gene"), P("gene", None), P("sample", "variant"), P())
    sizes = [mesh.shape[axis] for axis in ("gene", "sample", "variant")]
    return jax.shard_map(
        functools.partial(local, *sizes),
        mesh=mesh,
        in_specs=placed,
        out_specs=(P(("variant", "sample"), "gene"), P("sample", None)),
        check_vma=False,
    )
```

```python
import functools
import math

import jax
import jax.numpy as jnp
from jax import lax
from jax.experimental import pallas as pl
from jax.experimental.pallas import tpu as pltpu
from jax.sharding import PartitionSpec as P

F32 = jnp.float32
BF16 = jnp.bfloat16
VMEM_LIMIT = 32 << 20
LANES = 128
ROWS = 8
RHS_PIECES = 2


def round_up(n, m):
    return (n + m - 1) // m * m


def in_hbm(x):
    return pltpu.with_memory_space_constraint(x, pltpu.HBM)


def split3(x):
    hi = x.astype(BF16).astype(F32)
    rest = x - hi
    mid = rest.astype(BF16).astype(F32)
    return hi, mid, rest - mid


def stacked(parts, rows):
    have = sum(p.shape[0] for p in parts)
    if have < rows:
        parts = list(parts) + [jnp.zeros((rows - have, parts[0].shape[1]), F32)]
    return jnp.concatenate(parts, axis=0).astype(BF16)


def cholesky(entry, n):
    low = {}
    inv = []
    for j in range(n):
        d = entry(j, j)
        for k in range(j):
            d = d - low[j, k] * low[j, k]
        root = lax.rsqrt(d)
        root = root * (1.5 - 0.5 * d * root * root)
        inv.append(root)
        for i in range(j + 1, n):
            v = entry(i, j)
            for k in range(j):
                v = v - low[i, k] * low[j, k]
            low[i, j] = v * root
    return low, inv


def substitute(low, inv, right):
    n = len(right)
    y = []
    for i in range(n):
        v = right[i]
        for k in range(i):
            v = v - low[i, k] * y[k]
        y.append(v * inv[i])
    x = [None] * n
    for i in reversed(range(n)):
        v = y[i]
        for k in range(i + 1, n):
            v = v - low[k, i] * x[k]
        x[i] = v * inv[i]
    return x


def entries(tile):
    cache = {}

    def entry(i, j):
        if (i, j) not in cache:
            cache[i, j] = jnp.broadcast_to(tile[i : i + 1, j : j + 1], (ROWS, LANES))
        return cache[i, j]

    return entry


def inner_products(x, n):
    col = lax.broadcasted_iota(jnp.int32, (ROWS, LANES), 1)
    out = jnp.zeros((ROWS, LANES), F32)
    for j in range(n):
        out = jnp.where(col == j, jnp.sum(x * x[j : j + 1], axis=1, keepdims=True), out)
    return out


def wide(tile, like):
    rows, cols = like
    if rows == 1:
        return jnp.concatenate([tile[0:1]] * (cols // LANES), axis=1)
    return jnp.concatenate([tile] * (rows // ROWS), axis=0)


def rhs_kernel(
    types, halves, pieces, signature_in, profile_in, expression, held, parts, signature, profile, sems, few
):
    samples, genes = held.shape
    step = samples // pieces
    early = [
        pltpu.make_async_copy(signature_in, signature, few.at[0]),
        pltpu.make_async_copy(profile_in, profile, few.at[1]),
    ]
    for copy in early:
        copy.start()
    start = lax.rem(lax.axis_index("variant"), halves) * samples
    copies = []
    for i in range(pieces):
        rows = pl.ds(i * step, step)
        there = pl.ds(pl.multiple_of(start + i * step, step), step)
        copy = pltpu.make_async_copy(expression.at[there], held.at[rows], sems.at[i])
        copy.start()
        copies.append(copy)

    for copy in early:
        copy.wait()
    groups = genes // LANES
    base = lax.axis_index("gene") * genes
    shape = (groups, LANES)
    ids = (
        base
        + lax.broadcasted_iota(jnp.int32, shape, 0) * LANES
        + lax.broadcasted_iota(jnp.int32, shape, 1)
    )

    n_sig = signature.shape[0]
    unroll = 10 if n_sig % 10 == 0 else 1

    def look(i, member):
        for u in range(unroll):
            member = member | (ids == signature[i * unroll + u]).astype(jnp.int32)
        return member

    member = lax.fori_loop(0, n_sig // unroll, look, jnp.zeros(shape, jnp.int32))
    member = (member > 0).astype(F32)
    row = jnp.concatenate([member[h : h + 1] for h in range(groups)], axis=1)
    masked = profile[...] * row
    masked = jnp.concatenate([masked, jnp.zeros((ROWS - types, genes), F32)], axis=0)
    left = stacked(split3(masked), 32)
    parts[types * samples // LANES :, :] = inner_products(masked, types)

    for i in range(pieces):
        copies[i].wait()
        out = lax.dot_general(
            left,
            held[i * step : (i + 1) * step, :],
            (((1,), (1,)), ((), ())),
            preferred_element_type=F32,
        )
        out = out[0:ROWS] + (out[ROWS : 2 * ROWS] + out[2 * ROWS : 3 * ROWS])
        for c in range(step // LANES):
            at = (i * step // LANES + c) * types
            parts[at : at + types, :] = out[:types, c * LANES : (c + 1) * LANES]


def right_sides(expression, profile_t, signature, halves):
    samples, genes = expression.shape
    samples = samples // halves
    types = profile_t.shape[0]
    pieces = RHS_PIECES
    rows = types * samples // LANES + ROWS
    return pl.pallas_call(
        functools.partial(rhs_kernel, types, halves, pieces),
        in_specs=[pl.BlockSpec(memory_space=pltpu.HBM)] * 3,
        out_specs=[pl.BlockSpec(memory_space=pltpu.VMEM)] * 2,
        out_shape=[
            pltpu.VMEM((samples, genes), BF16),
            jax.ShapeDtypeStruct((rows, LANES), F32),
        ],
        scratch_shapes=[
            pltpu.SMEM(signature.shape, jnp.int32),
            pltpu.VMEM(profile_t.shape, F32),
            pltpu.SemaphoreType.DMA((pieces,)),
            pltpu.SemaphoreType.DMA((2,)),
        ],
        compiler_params=pltpu.CompilerParams(vmem_limit_bytes=VMEM_LIMIT),
        cost_estimate=pl.CostEstimate(
            flops=2 * 32 * samples * genes, bytes_accessed=2 * samples * genes, transcendentals=0
        ),
        name="right_sides",
    )(in_hbm(signature), in_hbm(profile_t), in_hbm(expression))


def prepare_kernel(own, halves, pieces, dosage_in, expression, first, rest, *refs):
    held = refs[:-3]
    dosage, sems, far_sem = refs[-3:]
    samples, variants = dosage.shape
    half = samples // halves
    step = samples // pieces
    side = lax.rem(lax.axis_index("variant"), halves)
    copies = []
    for i in range(pieces):
        near = i * step // half
        begin = lax.rem(side + near, halves) * half + (i * step - near * half)
        there = pl.ds(pl.multiple_of(begin, step), step)
        copy = pltpu.make_async_copy(dosage_in.at[there], dosage.at[pl.ds(i * step, step)], sems.at[i])
        copy.start()
        copies.append(copy)
    far = []
    for ref in held:
        there = pl.ds(pl.multiple_of((1 - side) * half, half), half)
        copy = pltpu.make_async_copy(expression.at[there], ref, far_sem)
        copy.start()
        far.append(copy)
    shift = lax.rem(variants - lax.axis_index("sample") * own, variants)
    for i in range(pieces):
        copies[i].wait()
        cols = slice(i * step, (i + 1) * step)
        turned = pltpu.roll(dosage[cols, :].astype(F32), shift, 1).T
        first[:, cols] = stacked([turned[:own]], first.shape[0])
        rest[:, cols] = stacked([turned[own:]], rest.shape[0])
    for copy in far:
        copy.wait()


def prepare(dosage, expression, own, halves):
    samples, variants = dosage.shape
    genes = expression.shape[1]
    pieces = 4
    first, rest = round_up(own, 16), round_up(variants - own, 16)
    return pl.pallas_call(
        functools.partial(prepare_kernel, own, halves, pieces),
        in_specs=[pl.BlockSpec(memory_space=pltpu.HBM)] * 2,
        out_specs=[pl.BlockSpec(memory_space=pltpu.VMEM)] * (1 + halves),
        out_shape=[pltpu.VMEM((first, samples), BF16), pltpu.VMEM((rest, samples), BF16)]
        + [pltpu.VMEM((samples // halves, genes), BF16)] * (halves - 1),
        scratch_shapes=[
            pltpu.VMEM(dosage.shape, jnp.int32),
            pltpu.SemaphoreType.DMA((pieces,)),
            pltpu.SemaphoreType.DMA,
        ],
        compiler_params=pltpu.CompilerParams(vmem_limit_bytes=VMEM_LIMIT),
        cost_estimate=pl.CostEstimate(
            flops=samples * variants, bytes_accessed=6 * samples * variants, transcendentals=0
        ),
        name="prepare",
    )(in_hbm(dosage), in_hbm(expression))


def solve_kernel(types, own_parts, x_parts, y_parts, d_parts, solved, packed):
    groups = (own_parts.shape[0] - ROWS) // types
    last = types * groups

    def total(rows):
        return (own_parts[rows, :] + x_parts[rows, :]) + (y_parts[rows, :] + d_parts[rows, :])

    low, inv = cholesky(entries(total(slice(last, last + ROWS))), types)
    like = (groups, LANES)
    low = {key: wide(value, like) for key, value in low.items()}
    inv = [wide(value, like) for value in inv]
    x = substitute(low, inv, [total(pl.ds(k, groups, stride=types)) for k in range(types)])
    for k in range(types):
        packed[pl.ds(k, groups, stride=ROWS), :] = x[k]
    for k in range(types, ROWS):
        packed[pl.ds(k, groups, stride=ROWS), :] = jnp.zeros(like, F32)
    for g in range(groups):
        solved[:, g * LANES : (g + 1) * LANES] = packed[g * ROWS : (g + 1) * ROWS, :]


def solve(parts, types):
    groups = (parts[0].shape[0] - ROWS) // types
    vmem = pl.BlockSpec(memory_space=pltpu.VMEM)
    return pl.pallas_call(
        functools.partial(solve_kernel, types),
        in_specs=[vmem] * 4,
        out_specs=vmem,
        out_shape=jax.ShapeDtypeStruct((ROWS, groups * LANES), F32),
        scratch_shapes=[pltpu.VMEM((groups * ROWS + ROWS, LANES), F32)],
        compiler_params=pltpu.CompilerParams(vmem_limit_bytes=VMEM_LIMIT),
        name="solve",
    )(*parts)


def design_rows(left, dosage, rounded, cols, count):
    types = len(rounded)
    width = rounded[0].shape[1]
    for k in range(types):
        spread = jnp.broadcast_to(rounded[k], (16, width)).astype(BF16)
        for q in range(count // 16):
            at = k * count + q * 16
            left[at : at + 16, :] = dosage[q * 16 : q * 16 + 16, cols] * spread


def others_kernel(types, step, first_col, has_before, *refs):
    p_in, mine, others, held = refs[:4]
    before = refs[4:8] if has_before else None
    cross, small, corr_own, corr_oth, left, weights = refs[-6:]
    samples, genes = held.shape
    n_rows = types * others.shape[0]

    pp = inner_products(p_in[...], types)
    small[ROWS:, :] = jnp.concatenate([pp, jnp.zeros((ROWS, genes - LANES), F32)], axis=1)
    if has_before:
        small[ROWS:, :LANES] += before[1][ROWS:, :LANES]

    for c in range(samples // step):
        here = slice(c * step, (c + 1) * step)
        cols = slice(first_col + c * step, first_col + (c + 1) * step)
        p = p_in[:, here]
        pieces = split3(p)
        rounded = [pieces[0][k : k + 1] for k in range(types)]
        design_rows(left, others, rounded, cols, others.shape[0])
        left[n_rows:, :] = stacked(pieces, 32)
        w = jnp.concatenate([r * p for r in rounded], axis=0)
        high = w.astype(BF16).astype(F32)
        weights[:64, :] = stacked([high], 64)
        weights[64:, :] = stacked([w - high], 64)
        out = jnp.dot(left[...], held[here, :], preferred_element_type=F32)
        contract = (((1,), (1,)), ((), ()))
        both = jnp.concatenate([others[:, cols], mine[:, cols]], axis=0)
        both = lax.dot_general(both, weights[...], contract, preferred_element_type=F32)
        co, cm = both[: others.shape[0]], both[others.shape[0] :]
        py = out[n_rows : n_rows + ROWS] + (
            out[n_rows + ROWS : n_rows + 2 * ROWS] + out[n_rows + 2 * ROWS : n_rows + 3 * ROWS]
        )
        old = None
        if c:
            old = (cross, small, corr_own, corr_oth)
        elif has_before:
            old = before
        if old is None:
            cross[...] = out[:n_rows]
            small[:ROWS, :] = py
            corr_own[...] = cm
            corr_oth[...] = co
        else:
            cross[...] = old[0][...] + out[:n_rows]
            small[:ROWS, :] = old[1][:ROWS, :] + py
            corr_own[...] = old[2][...] + cm
            corr_oth[...] = old[3][...] + co


def others_products(p, mine, others, held, first_col, before, types):
    samples, genes = held.shape
    step = 512
    n_mine, n_others = mine.shape[0], others.shape[0]
    vmem = pl.BlockSpec(memory_space=pltpu.VMEM)
    before = list(before or [])
    return pl.pallas_call(
        functools.partial(others_kernel, types, step, first_col, bool(before)),
        in_specs=[vmem] * (4 + len(before)),
        out_specs=[vmem] * 4,
        out_shape=[
            jax.ShapeDtypeStruct((types * n_others, genes), F32),
            jax.ShapeDtypeStruct((2 * ROWS, genes), F32),
            jax.ShapeDtypeStruct((n_mine, 128), F32),
            jax.ShapeDtypeStruct((n_others, 128), F32),
        ],
        scratch_shapes=[
            pltpu.VMEM((types * n_others + 32, step), BF16),
            pltpu.VMEM((128, step), BF16),
        ],
        compiler_params=pltpu.CompilerParams(vmem_limit_bytes=VMEM_LIMIT),
        cost_estimate=pl.CostEstimate(
            flops=2 * types * n_others * samples * genes,
            bytes_accessed=2 * samples * genes,
            transcendentals=0,
        ),
        name="others_products",
    )(p, mine, others, held, *before)


def own_dot(types, step, first_col, p_ref, mine, held, lanes, left, add, beside=None):
    count = held.shape[0] // step
    for c in range(count):
        here = slice(c * step, (c + 1) * step)
        cols = slice(first_col + c * step, first_col + (c + 1) * step)
        rounded = p_ref[:, here].astype(BF16).astype(F32)
        design_rows(left, mine, [rounded[k : k + 1] for k in range(types)], cols, mine.shape[0])
        if beside is not None:
            beside(c, count)
        add(jnp.dot(left[...], held[here, lanes], preferred_element_type=F32), first_col + c == 0)


def own_kernel(types, step, halves, *refs):
    p_in, held, mine = refs[:halves], refs[halves : 2 * halves], refs[2 * halves]
    cross, tail, left = refs[2 * halves + 1 :]
    half = p_in[0].shape[1]

    def add_to(total):
        def add(out, first):
            if first:
                total[...] = out
            else:
                total[...] += out

        return add

    columns, genes = cross.shape[1], held[0].shape[1]
    for i in range(halves):
        own_dot(types, step, i * half, p_in[i], mine, held[i], slice(0, columns), left, add_to(cross))
    own_dot(types, step, 0, p_in[0], mine, held[0], slice(columns, genes), left, add_to(tail))


def own_products(p, mine, held, columns, types):
    halves = len(p)
    samples, genes = halves * p[0].shape[1], held[0].shape[1]
    step = 1024
    rows = types * mine.shape[0]
    vmem = pl.BlockSpec(memory_space=pltpu.VMEM)
    return pl.pallas_call(
        functools.partial(own_kernel, types, step, halves),
        in_specs=[vmem] * (2 * halves + 1),
        out_specs=[vmem] * 2,
        out_shape=[
            jax.ShapeDtypeStruct((rows, columns), F32),
            jax.ShapeDtypeStruct((rows, genes - columns), F32),
        ],
        scratch_shapes=[pltpu.VMEM((rows, step), BF16)],
        compiler_params=pltpu.CompilerParams(vmem_limit_bytes=VMEM_LIMIT),
        cost_estimate=pl.CostEstimate(
            flops=2 * rows * samples * columns, bytes_accessed=2 * samples * columns, transcendentals=0
        ),
        name="own_products",
    )(*p, *held, mine)


def finish_kernel(types, step, scale, own, halves, peers, *refs):
    p_in, held, mine = refs[:halves], refs[halves : 2 * halves], refs[2 * halves]
    before, tail = refs[2 * halves + 1 : 2 * halves + 3]
    refs = refs[2 * halves + 3 :]
    smalls, corrs, blocks = refs[: 1 + peers], refs[1 + peers : 2 + 2 * peers], refs[2 + 2 * peers : 2 + 3 * peers]
    out, props_out, left, turned, last, ready, sems, props, props_sems = refs[2 + 3 * peers :]
    n_mine = mine.shape[0]
    genes, columns = held[0].shape[1], before.shape[1]

    half = p_in[0].shape[1]
    side = lax.rem(lax.axis_index("variant"), halves)
    copies = []
    for i in range(halves):
        at = pl.multiple_of(lax.rem(side + i, halves) * half, half)
        props[i] = p_in[i][:types, :]
        copy = pltpu.make_async_copy(props.at[i], props_out.at[:, pl.ds(at, half)], props_sems.at[i])
        copy.start()
        copies.append(copy)
    lanes = slice(columns, genes)

    seen = [tail]

    def add(out, first):
        last[...] = seen[-1][...] + out
        seen.append(last)

    small = smalls[0][...]
    corr = corrs[0][...]
    for i in range(peers):
        small = small + smalls[1 + i][...]
        corr = corr + corrs[1 + i][...]
    corr = corr[:, 0:64] + corr[:, 64:128]
    corr_t = corr.T
    low, inv = cholesky(entries(small[ROWS:, :LANES]), types)
    like = (1, genes)
    low = {key: wide(value, like) for key, value in low.items()}
    inv = [wide(value, like) for value in inv]
    coef = substitute(low, inv, [small[k : k + 1] for k in range(types)])
    coef = jnp.concatenate(coef + [jnp.zeros((ROWS - types, genes), F32)], axis=0)
    q = split3(coef)
    right = stacked([q[0], q[1], q[2], q[0], q[1], q[0]], 48)
    for k in range(types):
        c = split3(corr_t[ROWS * k : ROWS * (k + 1)])
        turned[:, k * n_mine : (k + 1) * n_mine] = jnp.concatenate(
            [c[0], c[0], c[0], c[1], c[1], c[2]], axis=0
        )
    turned_b = turned[...].T.astype(BF16)

    def write(t):
        tile = slice(t * LANES, (t + 1) * LANES)
        source, here = before, tile
        if t * LANES >= columns:
            source, here = seen[-1], slice(t * LANES - columns, (t + 1) * LANES - columns)
        fitted = jnp.dot(turned_b, right[:, tile], preferred_element_type=F32)
        for k in range(types):
            rows = slice(k * n_mine, k * n_mine + own)
            value = source[rows, here] - fitted[rows]
            for block in blocks:
                value = value + block[k * own : (k + 1) * own, tile]
            ready[t, pl.ds(k, own, stride=types), :] = value * scale
        copy = pltpu.make_async_copy(
            ready.at[t, pl.ds(0, types * own)], out.at[:, pl.ds(t * LANES, LANES)], sems.at[t]
        )
        copy.start()
        copies.append(copy)

    early, tiles = columns // LANES, genes // LANES

    def beside(c, count):
        for t in range(early * c // count, early * (c + 1) // count):
            write(t)

    for i in range(1, halves):
        own_dot(
            types, step, i * half, p_in[i], mine, held[i], lanes, left, add,
            beside if i == halves - 1 else None,
        )
    for t in range(early if halves > 1 else 0, tiles):
        write(t)
    for copy in copies:
        copy.wait()


def finish(p, mine, held, before, tail, smalls, corrs, blocks, own, types, scale):
    halves = len(p)
    genes, columns = held[0].shape[1], before.shape[1]
    step = 512
    rows = types * mine.shape[0]
    vmem = pl.BlockSpec(memory_space=pltpu.VMEM)
    return pl.pallas_call(
        functools.partial(finish_kernel, types, step, scale, own, halves, len(blocks)),
        in_specs=[vmem] * (2 * halves + 3 + 2 * len(smalls) + len(blocks)),
        out_specs=[pl.BlockSpec(memory_space=pl.ANY)] * 2,
        out_shape=[
            jax.ShapeDtypeStruct((types * own, genes), F32),
            jax.ShapeDtypeStruct((types, halves * p[0].shape[1]), F32),
        ],
        scratch_shapes=[
            pltpu.VMEM((rows, step), BF16),
            pltpu.VMEM((48, rows), F32),
            pltpu.VMEM((rows, genes - columns), F32),
            pltpu.VMEM((genes // LANES, types * own + ROWS, LANES), F32),
            pltpu.SemaphoreType.DMA((genes // LANES,)),
            pltpu.VMEM((halves, types, p[0].shape[1]), F32),
            pltpu.SemaphoreType.DMA((halves,)),
        ],
        compiler_params=pltpu.CompilerParams(vmem_limit_bytes=VMEM_LIMIT),
        name="finish",
    )(*p, *held, mine, before, tail, *smalls, *corrs, *blocks)


def exchange_all(part, n_gene):
    def swap(offset):
        return lax.ppermute(part, "gene", [(i, i ^ offset) for i in range(n_gene)])

    return (part, swap(2), swap(3), swap(1))


def local(n_gene, n_sample, n_variant, expression, profile, dosage, signature):
    s_dev, g_dev = expression.shape
    v_dev = dosage.shape[1]
    types = profile.shape[1]
    own = v_dev // n_sample
    scale = 1.0 / math.sqrt(s_dev * n_sample)
    halves = 2 if n_variant % 2 == 0 else 1
    half = s_dev // halves

    held, part = right_sides(expression, profile.T, signature, halves)
    parts = exchange_all(part, n_gene)
    mine, others, *far = prepare(dosage, expression, own, halves)
    held = [held] + far
    solved = [solve(parts, types)]
    if halves == 2:
        pairs = [(i, i ^ 1) for i in range(n_variant)]
        solved.append(lax.ppermute(solved[0], "variant", pairs))
    sums = None
    for i in range(halves):
        sums = others_products(solved[i], mine, others, held[i], i * half, sums, types)
    cross_oth, small, corr_own, corr_oth = sums
    n_mine, n_oth = mine.shape[0], others.shape[0]
    blocks, smalls, corrs = [], [small], [corr_own]
    for d in range(1, n_sample):
        pairs = [(i, (i + d) % n_sample) for i in range(n_sample)]
        cross, corr = cross_oth, corr_oth
        if n_oth != own:
            cut = slice((d - 1) * own, d * own)
            cross = cross.reshape(types, n_oth, g_dev)[:, cut].reshape(types * own, g_dev)
            corr = jnp.pad(corr[cut], ((0, n_mine - own), (0, 0)))
        smalls.append(lax.ppermute(small, "sample", pairs))
        corrs.append(lax.ppermute(corr, "sample", pairs))
        blocks.append(lax.ppermute(cross, "sample", pairs))
    columns = g_dev * 3 // 4 // LANES * LANES
    before, tail = own_products(solved, mine, held, columns, types)
    interaction, props_t = finish(
        solved, mine, held, before, tail, smalls, corrs, blocks, own, types, scale
    )
    return interaction, props_t.T


def solution(mesh):
    placed = (P("sample", "gene"), P("gene", None), P("sample", "variant"), P())
    sizes = [mesh.shape[axis] for axis in ("gene", "sample", "variant")]
    return jax.shard_map(
        functools.partial(local, *sizes),
        mesh=mesh,
        in_specs=placed,
        out_specs=(P(("variant", "sample"), "gene"), P("sample", None)),
        check_vma=False,
    )
```
